128 devices in a mesh: rows: 32 (over x, z, core), cols: 4 (over y).
Axes of the slice: x: 4, y: 4, z: 4, core: 2. Of those that a mesh axis runs over, the one named last changes fastest.
Arguments:
- momentum: bfloat16 [12288, 26624], P('rows', 'cols'), may hold values from -30 to 30
- gradient: bfloat16 [12288, 26624], P('rows', 'cols'), may hold values from -3 to 3
- basis: bfloat16 [512, 26624], P('rows', 'cols')
Outputs:
- momentum_new: bfloat16 [12288, 26624], P('rows', 'cols')
- basis_new: bfloat16 [512, 26624], P('rows', 'cols')
- update: bfloat16 [12288, 26624], P('rows', 'cols')
The draws below stay inside these ranges and needn't reach their ends.
All inputs are finite; a program needn't handle non-finite values.
Results may differ from the reference program's by a relative error of at most 0.027.
Values may be sent and summed in bfloat16 or wider, within the bound.
A program may use at most 128 MiB of HBM per device.

```python
import math
import jax
import jax.numpy as jnp
from jax import lax

ROWS = 12288
WIDTH = 26624
RANK = 512
N_ROWS = 32


def shared_basis(key):
    normals = jax.random.normal(jax.random.fold_in(key, 101), (RANK, WIDTH), jnp.float32)
    return jnp.clip(normals, -4.5, 4.5) / math.sqrt(WIDTH)


def draw_basis(key, part):
    common = shared_basis(key)
    return common.astype(jnp.bfloat16)


def draw_momentum(key, part):
    common = shared_basis(key)
    key = jax.random.fold_in(key, 11)
    key_rows, key_cols, key_mix, key_vals = jax.random.split(key, 4)
    row_ramp = jnp.exp(0.5 * math.log(3.0) * jnp.arange(ROWS, dtype=jnp.float32) / ROWS)
    col_ramp = jnp.exp(0.5 * math.log(3.0) * jnp.arange(WIDTH, dtype=jnp.float32) / WIDTH)
    row_scale = jnp.exp(jax.random.uniform(key_rows, (ROWS,), jnp.float32, 0.0, math.log(4.0))) * row_ramp
    col_scale = jnp.exp(jax.random.uniform(key_cols, (WIDTH,), jnp.float32, 0.0, math.log(4.0))) * col_ramp
    mixing = jax.random.normal(key_mix, (ROWS, RANK), jnp.float32)
    signal = jnp.dot(mixing, common, precision=lax.Precision.HIGHEST) * math.sqrt(WIDTH / RANK)
    noise = jnp.clip(jax.random.normal(key_vals, (ROWS, WIDTH), jnp.float32), -6.0, 6.0)
    values = 0.25 * signal + 0.05 * noise
    scaled = values * row_scale[:, None] * col_scale[None, :]
    return jnp.clip(scaled, -30.0, 30.0).astype(jnp.bfloat16)


def shard_levels(key, extent, cuts, least, top_value):
    def one(axis_at, shards_of):
        heights = jax.random.uniform(jax.random.fold_in(jax.random.fold_in(key, 6), axis_at), (shards_of,), jnp.float32, least / len(cuts), top_value / len(cuts))
        return jnp.repeat(jnp.exp(heights), extent[axis_at] // shards_of).reshape((-1,) + (1,) * (len(extent) - axis_at - 1))

    factor_of = one(*cuts[0])
    for cut in cuts[1:]:
        factor_of = factor_of * one(*cut)
    return factor_of


def gaussian(own_key, extent, spread, reach, cuts=(), kind=jnp.bfloat16):
    level = shard_levels(own_key, extent, cuts, -0.22, 0.18) if cuts else 1.0
    entries = jax.random.normal(own_key, extent, jnp.float32) * spread * level
    return jnp.minimum(jnp.maximum(entries, -reach), reach).astype(kind)


def setup_inputs(seed: int = 0) -> dict:
    seeds = jax.random.split(jax.random.key(seed), 4)
    return {
        "momentum": draw_momentum(jax.random.fold_in(seeds[3], 71), 0),
        "gradient": gaussian(seeds[1], (ROWS, WIDTH), 0.5, 3.0, ((0, 32), (1, 4))),
        "basis": draw_basis(jax.random.fold_in(seeds[3], 71), 0),
    }


def reference(momentum, gradient, basis):
    buffer = (momentum.astype(jnp.float32) + gradient.astype(jnp.float32)).astype(jnp.bfloat16)
    left = lax.dot_general(buffer.astype(jnp.float32), basis.astype(jnp.float32), (((1,), (1,)), ((), ())), preferred_element_type=jnp.float32)
    gram = jnp.dot(left.T, left, precision=lax.Precision.HIGHEST)
    lower = jnp.linalg.cholesky(gram)
    ortho = jax.scipy.linalg.solve_triangular(lower, left.T, lower=True).T.astype(jnp.bfloat16)
    block_rows = ROWS // N_ROWS
    buffer_blocks = buffer.reshape(N_ROWS, block_rows, WIDTH)
    ortho_blocks = ortho.reshape(N_ROWS, block_rows, RANK)

    def accumulate(carry, pieces):
        part = lax.dot_general(pieces[1].astype(jnp.float32), pieces[0].astype(jnp.float32), (((0,), (0,)), ((), ())), preferred_element_type=jnp.float32)
        rounded = lax.optimization_barrier(part.astype(jnp.bfloat16))
        return (carry + rounded.astype(jnp.float32), None)
    start = jnp.zeros((RANK, WIDTH), jnp.float32)
    total, unused = lax.scan(accumulate, start, (buffer_blocks, ortho_blocks))
    right = total.astype(jnp.bfloat16)
    right_wide = right.astype(jnp.float32)
    norms = jnp.sqrt(lax.optimization_barrier(jnp.sum(right_wide * right_wide, axis=1)) + 1e-06)
    basis_new = (right_wide / norms[:, None]).astype(jnp.bfloat16)
    feedback = jnp.dot(ortho.astype(jnp.float32), right.astype(jnp.float32), preferred_element_type=jnp.float32)
    momentum_new = (buffer.astype(jnp.float32) - 0.2 * feedback).astype(jnp.bfloat16)
    factor = math.sqrt(ROWS * WIDTH / RANK)
    update = (factor * jnp.dot(ortho.astype(jnp.float32), basis_new.astype(jnp.float32), preferred_element_type=jnp.float32)).astype(jnp.bfloat16)
    return (momentum_new, basis_new, update)
```

```python
import functools
import math

import jax
import jax.numpy as jnp
from jax import lax
from jax.experimental import pallas as pl
from jax.experimental.pallas import tpu as pltpu
from jax.sharding import PartitionSpec as P

ROWS = 12288
WIDTH = 26624
RANK = 512
MESH = pl.DeviceIdType.MESH
BF = jnp.bfloat16
F32 = jnp.float32

LOCAL = 384
COLS = 6656
HALF = 3328
PART = 1664
SEG = 832
SUB = 208
B = 128
N_SEMS = 192


def mod4(v):
    return lax.rem(v + 4, 4)


def rows_at(start, size, unit=16):
    return pl.ds(pl.multiple_of(start, unit), size)


def dotp(a, b, dims):
    return lax.dot_general(
        a, b, (dims, ((), ())), precision=lax.Precision.HIGHEST, preferred_element_type=F32
    )


def dotb(a, b, dims):
    return lax.dot_general(a, b, (dims, ((), ())), preferred_element_type=F32)


def split(a):
    hi = a.astype(BF)
    return hi, (a - hi.astype(F32)).astype(BF)


def sweep(w_ref, t, hook):
    sub = lax.broadcasted_iota(jnp.int32, (8, B), 0)
    lane = lax.broadcasted_iota(jnp.int32, (8, B), 1)
    panels = B // 8
    for p in range(panels):
        top = t[:8]
        cols = jnp.stack(
            [jnp.broadcast_to(top[:, 8 * p + j : 8 * p + j + 1], (8, B)) for j in range(8)]
        )
        for j in range(8):
            inv = lax.rsqrt(jnp.broadcast_to(cols[j, j : j + 1, :], (8, B)))
            below = jnp.where(sub > j, cols[j] * inv, 0.0)
            own = jnp.where(sub > j, 0.0, jnp.where(sub == j, 1.0, cols[j]))
            parts = [cols[:j]] if j else []
            parts.append(own[None])
            if j < 7:
                parts.append(cols[j + 1 :])
            cols = jnp.concatenate(parts, axis=0)
            row = cols[:, j : j + 1, :] * inv[None]
            cols = jnp.where((sub == j)[None], row, cols - below[None] * row)
        tri = [jnp.where(sub >= k, cols[k], 0.0) for k in range(8)]
        inside = (lane >= 8 * p) & (lane < 8 * p + 8)
        eye = jnp.where(inside, jnp.where(lane - 8 * p == sub, 1.0, 0.0), top)
        new = tri[0] * eye[0:1]
        for k in range(1, 8):
            new = new + tri[k] * eye[k : k + 1]
        w_ref[8 * p : 8 * p + 8, :] = jnp.where(lane <= sub + 8 * p, new, 0.0)
        if p < panels - 1:
            rest = t[8:]
            lanes = lax.broadcasted_iota(jnp.int32, rest.shape, 1)
            t = jnp.where((lanes >= 8 * p) & (lanes < 8 * p + 8), 0.0, rest)
            for k in range(8):
                y = jnp.sum(tri[k] * new, axis=0, keepdims=True)
                t = t - rest[:, 8 * p + k : 8 * p + k + 1] * y
        if p % 4 == 3:
            hook(p // 4)


def chol_inv(t_ref, w_ref, hook):
    lanes = lax.broadcasted_iota(jnp.int32, (B, RANK), 1)
    subs = lax.broadcasted_iota(jnp.int32, (B, RANK), 0)

    def block(k, carry):
        base = pl.multiple_of(k * B, B)
        rows = pl.ds(base, B)
        sweep(w_ref, t_ref[rows, rows], functools.partial(hook, k))
        own = (lanes >= base) & (lanes < base + B)
        mine = jnp.where(own, jnp.where(lanes - base == subs, 1.0, 0.0), t_ref[rows, :])
        new = dotp(w_ref[...], mine, ((1,), (0,)))
        t_ref[rows, :] = new

        def below(i, c):
            at = pl.ds(pl.multiple_of(i * B, B), B)
            t_ref[at, :] = jnp.where(own, 0.0, t_ref[at, :]) - dotp(
                t_ref[rows, at], new, ((0,), (0,))
            )
            return c

        lax.fori_loop(k + 1, RANK // B, below, 0)
        return carry

    lax.fori_loop(0, RANK // B, block, 0)


def gather_kernel(
    m_hbm, g_hbm, basis_hbm, zt_hbm, lhs_ref,
    mbuf, gbuf, sbuf, buf2, buf2t, bas, pleft, psend, precv, cp, yrh, yrf, left2,
    gs, gr, gram, tmat, wmat, zp, zown, zrh, zrf, zr2, zfull, nr1, nr2,
    load_sem, send_sem, recv_sem,
):
    r = lax.axis_index("rows")
    y = lax.axis_index("cols")
    c = lax.rem(r, 2)
    z = lax.rem(lax.div(r, 2), 4)
    x = lax.div(r, 8)
    p1 = x * (1 - c) + z * c
    p2 = z * (1 - c) + x * c

    def chip(a, b):
        return a * (4 - 3 * c) + b * (1 + 3 * c)

    def device(a, b):
        return 2 * chip(a, b) + c

    sib = (r + 1 - 2 * c, y)
    a1p = (device(mod4(p1 + 1), p2), y)
    a1m = (device(mod4(p1 - 1), p2), y)
    a2p = (device(p1, mod4(p2 + 1)), y)
    a2m = (device(p1, mod4(p2 - 1)), y)
    yp = (r, mod4(y + 1))
    ym = (r, mod4(y - 1))
    plane = [(dx, dz) for dx in range(4) for dz in range(4) if dx or dz]

    def peer(dx, dz):
        return (mod4(x + dx) * 8 + mod4(z + dz) * 2 + c, y)

    def source_chip(dx, dz):
        return mod4(x - dx) * 4 + mod4(z - dz)

    group = [(dy, dc) for dy in range(4) for dc in range(2) if dy or dc]

    def member(dy, dc):
        return (r + dc * (1 - 2 * c), mod4(y + dy))

    count = [0]
    sent = []

    def plan(src, dst, to, landing):
        i = count[0]
        count[0] += 1

        def copy(s, d):
            return pltpu.make_async_remote_copy(
                s, d, send_sem.at[i], recv_sem.at[i], device_id=to, device_id_type=MESH
            )

        sent.append(lambda: copy(src, dst).wait_send())
        return (lambda: copy(src, dst).start()), (lambda: copy(landing, landing).wait_recv())

    def send(src, dst, to, landing):
        start, wait = plan(src, dst, to, landing)
        start()
        return wait

    def columns(core, part):
        return pl.ds(pl.multiple_of(core * HALF + part * PART, 128), PART)

    order = [(1 - c, 0), (1 - c, 1), (c, 0), (c, 1)]

    def load(n):
        at = columns(*order[n])
        return [
            pltpu.make_async_copy(m_hbm.at[:, at], mbuf.at[n % 2], load_sem.at[2 * n]),
            pltpu.make_async_copy(g_hbm.at[:, at], gbuf.at[n % 2], load_sem.at[2 * n + 1]),
        ]

    loads = [load(n) for n in range(4)]
    for n in range(2):
        for copy in loads[n]:
            copy.start()
    own_rows = rows_at(r * 16, 16)
    parts = [pl.ds(0, PART), pl.ds(PART, PART)]
    own_basis = [
        pltpu.make_async_copy(
            basis_hbm.at[:, columns(c, n)], bas.at[own_rows, parts[n]], load_sem.at[8 + n]
        )
        for n in range(2)
    ]
    for copy in own_basis:
        copy.start()

    barrier = pltpu.get_barrier_semaphore()
    others = [peer(*d) for d in plane] + [member(*d) for d in group]
    for to in others:
        pl.semaphore_signal(barrier, inc=1, device_id=to, device_id_type=MESH)
    pl.semaphore_wait(barrier, len(others))

    sib_rows = rows_at((r + 1 - 2 * c) * 16, 16)
    got = [
        send(
            basis_hbm.at[:, columns(1 - c, n)],
            bas.at[own_rows, parts[n]],
            sib,
            bas.at[sib_rows, parts[n]],
        )
        for n in range(2)
    ]

    def piece(a, b, n):
        return bas.at[rows_at(chip(a, b) * 32, 32), parts[n]]

    def half_piece(a, b, n, h):
        return bas.at[rows_at(chip(a, b) * 32 + 16 * h, 16), parts[n]]

    def at1(d):
        return mod4(p1 + d)

    def at2(d):
        return mod4(p2 + d)

    first = []
    for n in range(2):
        own_basis[n].wait()
        got[n]()
        mine = piece(p1, p2, n)
        first.append(
            (
                send(mine, mine, a1p, piece(at1(-1), p2, n)),
                send(mine, mine, a1m, piece(at1(1), p2, n)),
            )
        )

    def both2(a, n):
        ref = piece(a, p2, n)
        return (
            send(ref, ref, a2p, piece(a, at2(-1), n)),
            send(ref, ref, a2m, piece(a, at2(1), n)),
        )

    def add_loaded(n, dst, row0, col0):
        for copy in loads[n]:
            copy.wait()

        def step(i, carry):
            at = rows_at(i * 16, 16)
            total = mbuf[n % 2, at, :].astype(F32) + gbuf[n % 2, at, :].astype(F32)
            dst[rows_at(row0 + i * 16, 16), pl.ds(col0, PART)] = total.astype(BF)
            return carry

        lax.fori_loop(0, LOCAL // 16, step, 0)
        if n < 2:
            for copy in loads[n + 2]:
                copy.start()

    my_rows = rows_at(c * LOCAL, LOCAL, 128)
    sib_side = rows_at((1 - c) * LOCAL, LOCAL, 128)

    def send_buffer(n):
        return send(
            sbuf.at[:, parts[n]], buf2.at[my_rows, parts[n]], sib, buf2.at[sib_side, parts[n]]
        )

    def turn(n, core):
        side = rows_at(core * LOCAL, LOCAL, 128)

        def step(i, carry):
            at = rows_at(n * PART + i * 128, 128, 128)
            buf2t[at, side] = buf2[side, at].T
            return carry

        lax.fori_loop(0, PART // 128, step, 0)

    add_loaded(0, sbuf, 0, 0)
    swapped = [send_buffer(0)]
    second = [[], []]
    opposite1 = []
    for n in range(2):
        from_m, from_p = first[n]
        second[n].append(both2(p1, n))
        from_m()
        ref = half_piece(at1(-1), p2, n, 0)
        opp0 = send(ref, ref, a1p, half_piece(at1(2), p2, n, 0))
        second[n].append(both2(at1(-1), n))
        from_p()
        ref = half_piece(at1(1), p2, n, 1)
        opp1 = send(ref, ref, a1m, half_piece(at1(2), p2, n, 1))
        second[n].append(both2(at1(1), n))
        opposite1.append((opp0, opp1))
    add_loaded(1, sbuf, 0, PART)
    swapped.append(send_buffer(1))
    for n in range(2):
        for wait in opposite1[n]:
            wait()
        second[n].append(both2(at1(2), n))
    add_loaded(2, buf2, c * LOCAL, 0)
    last = [[], []]
    offsets = (0, -1, 1, 2)

    def forward2(n, q):
        a = at1(offsets[q])
        from_m, from_p = second[n][q]
        from_m()
        ref = half_piece(a, at2(-1), n, 0)
        last[n].append(send(ref, ref, a2p, half_piece(a, at2(2), n, 0)))
        from_p()
        ref = half_piece(a, at2(1), n, 1)
        last[n].append(send(ref, ref, a2m, half_piece(a, at2(2), n, 1)))

    forward2(0, 0)
    forward2(0, 1)
    add_loaded(3, buf2, c * LOCAL, PART)
    forward2(0, 2)
    forward2(0, 3)
    forward2(1, 0)
    turn(0, c)
    forward2(1, 1)
    turn(1, c)
    swapped[0]()
    turn(0, 1 - c)
    forward2(1, 2)
    swapped[1]()
    turn(1, 1 - c)
    forward2(1, 3)

    for wait in last[0]:
        wait()
    pleft[sib_side, :] = dotb(buf2[sib_side, parts[0]], bas[:, parts[0]], ((1,), (1,)))
    pleft[my_rows, :] = dotb(buf2[my_rows, parts[0]], bas[:, parts[0]], ((1,), (1,)))
    for wait in last[1]:
        wait()
    psend[...] = (
        pleft[sib_side, :] + dotb(buf2[sib_side, parts[1]], bas[:, parts[1]], ((1,), (1,)))
    ).astype(BF)
    paired = send(psend, precv, sib, precv)
    pleft[my_rows, :] += dotb(buf2[my_rows, parts[1]], bas[:, parts[1]], ((1,), (1,)))
    paired()

    def ring_sum(plus, minus, size, value, out, half_in, full_in, between):
        half = size // 2

        def put(d, h, extra):
            v = value(d, h)
            if extra is not None:
                v = v + extra[...].astype(F32)
            slot = out.at[d % 4, h]
            slot[...] = v.astype(BF)
            return slot

        h0 = send(put(2, 0, None), half_in.at[0], plus, half_in.at[0])
        h1 = send(put(2, 1, None), half_in.at[1], minus, half_in.at[1])
        waits = [
            send(put(1, 1, None), full_in.at[0, 1], plus, full_in.at[0, 1]),
            send(put(-1, 0, None), full_in.at[1, 0], minus, full_in.at[1, 0]),
        ]
        between()
        h0()
        waits.append(send(put(1, 0, half_in.at[0]), full_in.at[0, 0], plus, full_in.at[0, 0]))
        h1()
        waits.append(send(put(-1, 1, half_in.at[1]), full_in.at[1, 1], minus, full_in.at[1, 1]))
        return waits

    def left_value(d, h):
        at = mod4(y + d) * 96 + 48 * h
        return pleft[rows_at(c * LOCAL + at, 48), :] + precv[rows_at(at, 48), :].astype(F32)

    waits = ring_sum(yp, ym, 96, left_value, cp, yrh, yrf, lambda: None)
    for wait in waits:
        wait()

    def left_rows(core, d, h=None):
        start = core * LOCAL + mod4(y + d) * 96
        if h is None:
            return left2.at[rows_at(start, 96)]
        return left2.at[rows_at(start + 48 * h, 48)]

    for h in range(2):
        total = left_value(0, h) + yrf[0, h].astype(F32) + yrf[1, h].astype(F32)
        left2[rows_at(c * LOCAL + y * 96 + 48 * h, 48), :] = total.astype(BF)
    mine = left_rows(c, 0)
    from_m = send(mine, mine, yp, left_rows(c, -1))
    from_p = send(mine, mine, ym, left_rows(c, 1))
    pair = [send(mine, mine, sib, left_rows(1 - c, 0))]
    from_m()
    ref = left_rows(c, -1, 0)
    opp0 = send(ref, ref, yp, left_rows(c, 2, 0))
    ref = left_rows(c, -1)
    pair.append(send(ref, ref, sib, left_rows(1 - c, -1)))
    from_p()
    ref = left_rows(c, 1, 1)
    opp1 = send(ref, ref, ym, left_rows(c, 2, 1))
    ref = left_rows(c, 1)
    pair.append(send(ref, ref, sib, left_rows(1 - c, 1)))
    opp0()
    opp1()
    ref = left_rows(c, 2)
    pair.append(send(ref, ref, sib, left_rows(1 - c, 2)))
    for wait in pair:
        wait()

    gs[...] = dotb(left2[:, rows_at(y * 128, 128, 128)], left2[...], ((0,), (0,)))

    def tile(base, j):
        return (
            rows_at(base + lax.div(j, 2) * 8, 8, 8),
            rows_at(lax.rem(j, 2) * 256, 256, 128),
        )

    j_me = x * 4 + z
    gram_in = []
    for e, (dx, dz) in enumerate(plane):
        rr, cc = tile(c * 64, mod4(x + dx) * 4 + mod4(z + dz))
        gram_in.append(send(gs.at[rr, cc], gr.at[e], peer(dx, dz), gr.at[e]))
    state = {}

    def gram_steps():
        for wait in gram_in:
            wait()
        rr, cc = tile(c * 64, j_me)
        total = gs[rr, cc]
        for e in range(15):
            total = total + gr[e]
        base = y * 128 + c * 64
        rr, cc = tile(base, j_me)
        gram[rr, cc] = total
        waits = []
        for dx, dz in plane:
            ref = gram.at[rr, cc]
            waits.append(
                send(ref, ref, peer(dx, dz), gram.at[tile(base, source_chip(dx, dz))])
            )
        state["gather"] = waits

    def z_value(d, h):
        at = rows_at(mod4(p1 + d) * SEG + (SEG // 2) * h, SEG // 2)
        return dotb(buf2t[at, :], left2[...], ((1,), (0,)))

    def gram_rows(core, d, h=None):
        start = mod4(y + d) * 128 + core * 64
        if h is None:
            return gram.at[rows_at(start, 64)]
        return gram.at[rows_at(start + 32 * h, 32)]

    def between():
        gram_steps()
        for h in range(2):
            zown[h] = z_value(0, h)
        for wait in state["gather"]:
            wait()
        mine = gram_rows(c, 0)
        state["m"] = send(mine, mine, yp, gram_rows(c, -1))
        state["p"] = send(mine, mine, ym, gram_rows(c, 1))
        state["pair"] = [send(mine, mine, sib, gram_rows(1 - c, 0))]

    z_waits = ring_sum(a1p, a1m, SEG, z_value, zp, zrh, zrf, between)
    state["m"]()
    ref = gram_rows(c, -1, 0)
    opp0 = send(ref, ref, yp, gram_rows(c, 2, 0))
    ref = gram_rows(c, -1)
    pair = state["pair"]
    pair.append(send(ref, ref, sib, gram_rows(1 - c, -1)))
    state["p"]()
    ref = gram_rows(c, 1, 1)
    opp1 = send(ref, ref, ym, gram_rows(c, 2, 1))
    ref = gram_rows(c, 1)
    pair.append(send(ref, ref, sib, gram_rows(1 - c, 1)))
    opp0()
    opp1()
    ref = gram_rows(c, 2)
    pair.append(send(ref, ref, sib, gram_rows(1 - c, 2)))
    for wait in pair:
        wait()
    tmat[...] = gram[...]

    def sub_rows(a, b):
        return rows_at(a * SEG + b * SUB, SUB)

    def sub_half(a, b, h):
        return rows_at(a * SEG + b * SUB + 112 * h, 112 - 16 * h)

    def to_sib(rows, landing):
        return plan(
            zfull.at[rows],
            zt_hbm.at[rows_at(c * HALF + rows.start, rows.size)],
            sib,
            zt_hbm.at[rows_at((1 - c) * HALF + landing.start, rows.size)],
        )

    def part(b):
        return zp.at[0, lax.div(b, 2), rows_at(lax.rem(b, 2) * SUB, SUB)]

    own = zfull.at[sub_rows(p1, p2)]
    z2, z3, z4, z5, zs = {}, {}, {}, {}, {}
    for d in (2, 1, 3):
        to = (device(p1, at2(d)), y)
        z2[d] = plan(part(at2(d)), zr2.at[d - 1], to, zr2.at[d - 1])
        z3[d] = plan(own, own, to, zfull.at[sub_rows(p1, at2(-d))])
    for d in range(4):
        b = at2(d)
        ref = zfull.at[sub_rows(p1, b)]
        z4[d] = (
            plan(ref, ref, a1p, zfull.at[sub_rows(at1(-1), b)]),
            plan(ref, ref, a1m, zfull.at[sub_rows(at1(1), b)]),
        )
        ref, ref1 = zfull.at[sub_half(at1(-1), b, 0)], zfull.at[sub_half(at1(1), b, 1)]
        z5[d] = (
            plan(ref, ref, a1p, zfull.at[sub_half(at1(2), b, 0)]),
            plan(ref1, ref1, a1m, zfull.at[sub_half(at1(2), b, 1)]),
        )
        for a in range(4):
            zs[a, d] = to_sib(sub_rows(at1(a), b), sub_rows(at2(a), at1(d)))

    def z_sum1():
        for wait in z_waits:
            wait()
        for h in range(2):

            def step(i, carry):
                at = rows_at(i * 16, 16)
                total = zown[h, at, :] + zrf[0, h, at, :].astype(F32)
                total = total + zrf[1, h, at, :].astype(F32)
                zp[0, h, at, :] = total.astype(BF)
                return carry

            lax.fori_loop(0, SEG // 32, step, 0)
        for start, _ in z2.values():
            start()

    def z_out(d):
        z4[d][0][0]()
        z4[d][1][0]()
        zs[0, d][0]()

    def z_sum2():
        for _, wait in z2.values():
            wait()

        def step(i, carry):
            at = rows_at(i * 16, 16)
            mine = rows_at(lax.rem(p2, 2) * SUB + i * 16, 16)
            total = zp[0, lax.div(p2, 2), mine, :].astype(F32)
            for d in range(3):
                total = total + zr2[d, at, :].astype(F32)
            zfull[rows_at(p1 * SEG + p2 * SUB + i * 16, 16), :] = total.astype(BF)
            return carry

        lax.fori_loop(0, SUB // 16, step, 0)
        for start, _ in z3.values():
            start()
        z_out(0)

    def z_gather2(d):
        z3[d][1]()
        z_out((4 - d) % 4)

    def z_forward(d):
        (_, from_m), (_, from_p) = z4[d]
        from_m()
        z5[d][0][0]()
        zs[3, d][0]()
        from_p()
        z5[d][1][0]()
        zs[1, d][0]()

    def z_last(d):
        for _, wait in z5[d]:
            wait()
        zs[2, d][0]()

    steps = {
        (0, 3): z_sum1,
        (2, 0): z_sum2,
        (3, 1): lambda: z_gather2(1),
        (3, 2): lambda: z_gather2(3),
        (3, 3): lambda: z_gather2(2),
    }

    def hook(k, part):
        for (at, which), step in steps.items():
            if which == part:
                pl.when(k == at)(step)

    chol_inv(tmat, wmat, hook)
    ri = lax.broadcasted_iota(jnp.int32, (RANK, RANK), 0)
    ci = lax.broadcasted_iota(jnp.int32, (RANK, RANK), 1)
    tmat[...] = jnp.where(ci <= ri, tmat[...], 0.0)
    w_hi, w_lo = split(tmat[...])

    shard = zfull[sub_rows(p1, p2), :]
    right = dotb(shard, w_hi, ((1,), (1,))) + dotb(shard, w_lo, ((1,), (1,)))
    nr1[0] = jnp.sum((right * right).reshape(SUB // 8, 8, RANK), axis=0)
    norm_in = [
        send(nr1.at[0], nr1.at[e + 1], peer(dx, dz), nr1.at[e + 1])
        for e, (dx, dz) in enumerate(plane)
    ]
    z_forward(0)
    own_left = left2[my_rows, :]
    ortho = (dotb(own_left, w_hi, ((1,), (1,))) + dotb(own_left, w_lo, ((1,), (1,)))).astype(BF)
    lhs_ref[0:LOCAL, :] = (
        dotb(ortho, w_hi, ((1,), (0,))) + dotb(ortho, w_lo, ((1,), (0,)))
    ).astype(BF)
    for wait in norm_in:
        wait()
    total = nr1[0]
    for e in range(15):
        total = total + nr1[e + 1]
    nr2[0] = total
    norm_in = [
        send(nr2.at[0], nr2.at[f + 1], member(dy, dc), nr2.at[f + 1])
        for f, (dy, dc) in enumerate(group)
    ]
    z_forward(3)
    z_forward(1)
    for wait in norm_in:
        wait()
    total = nr2[0]
    for f in range(7):
        total = total + nr2[f + 1]
    scale = lax.rsqrt(jnp.sum(total, axis=0, keepdims=True) + 1e-06)
    sub16 = lax.broadcasted_iota(jnp.int32, (16, RANK), 0)
    lane16 = lax.broadcasted_iota(jnp.int32, (16, RANK), 1)
    pick = jnp.where(lane16 == sub16 + r * 16, scale, 0.0)
    o_hi, o_lo = split(jnp.concatenate([ortho.astype(F32) * scale, pick], axis=0))
    lhs_ref[LOCAL : 2 * LOCAL + 16, :] = (
        dotb(o_hi, w_hi, ((1,), (0,)))
        + (dotb(o_hi, w_lo, ((1,), (0,))) + dotb(o_lo, w_hi, ((1,), (0,))))
    ).astype(BF)
    z_forward(2)
    for d in (0, 3, 1, 2):
        z_last(d)
    out = pltpu.make_async_copy(zfull, zt_hbm.at[rows_at(c * HALF, HALF)], load_sem.at[10])
    out.start()
    for _, wait in zs.values():
        wait()
    out.wait()
    for wait in sent:
        wait()


def gather_call(momentum, gradient, basis):
    anyspace = pl.BlockSpec(memory_space=pl.ANY)
    vmem = pl.BlockSpec(memory_space=pltpu.VMEM)
    scratch = [
        ((2, LOCAL, PART), BF),
        ((2, LOCAL, PART), BF),
        ((LOCAL, HALF), BF),
        ((2 * LOCAL, HALF), BF),
        ((HALF, 2 * LOCAL), BF),
        ((RANK, HALF), BF),
        ((2 * LOCAL, RANK), F32),
        ((LOCAL, RANK), BF),
        ((LOCAL, RANK), BF),
        ((4, 2, 48, RANK), BF),
        ((2, 48, RANK), BF),
        ((2, 2, 48, RANK), BF),
        ((2 * LOCAL, RANK), BF),
        ((128, RANK), F32),
        ((15, 8, 256), F32),
        ((RANK, RANK), F32),
        ((RANK, RANK), F32),
        ((B, B), F32),
        ((4, 2, SEG // 2, RANK), BF),
        ((2, SEG // 2, RANK), F32),
        ((2, SEG // 2, RANK), BF),
        ((2, 2, SEG // 2, RANK), BF),
        ((3, SUB, RANK), BF),
        ((HALF, RANK), BF),
        ((16, 8, RANK), F32),
        ((8, 8, RANK), F32),
    ]
    return pl.pallas_call(
        gather_kernel,
        out_shape=(
            jax.ShapeDtypeStruct((COLS, RANK), BF),
            jax.ShapeDtypeStruct((2 * LOCAL + 16, RANK), BF),
        ),
        in_specs=[anyspace] * 3,
        out_specs=(anyspace, vmem),
        scratch_shapes=[pltpu.VMEM(s, t) for s, t in scratch]
        + [
            pltpu.SemaphoreType.DMA((11,)),
            pltpu.SemaphoreType.DMA((N_SEMS,)),
            pltpu.SemaphoreType.DMA((N_SEMS,)),
        ],
        compiler_params=pltpu.CompilerParams(
            collective_id=0, has_side_effects=True, vmem_limit_bytes=56 << 20
        ),
        name="project",
    )(momentum, gradient, basis)


def apply_kernel(m_ref, g_ref, zt_ref, lhs_ref, mom_ref, bas_ref, upd_ref):
    prod = dotb(lhs_ref[...], zt_ref[...], ((1,), (1,)))
    total = (m_ref[...].astype(F32) + g_ref[...].astype(F32)).astype(BF).astype(F32)
    mom_ref[...] = (total - 0.2 * prod[:LOCAL]).astype(BF)
    factor = math.sqrt(ROWS * WIDTH / RANK)
    upd_ref[...] = (factor * prod[LOCAL : 2 * LOCAL]).astype(BF)
    bas_ref[...] = prod[2 * LOCAL :].astype(BF)


def apply_call(momentum, gradient, zt, lhs):
    wide = 512
    block = pl.BlockSpec((LOCAL, wide), lambda i: (0, i))
    return pl.pallas_call(
        apply_kernel,
        grid=(COLS // wide,),
        out_shape=(
            jax.ShapeDtypeStruct((LOCAL, COLS), BF),
            jax.ShapeDtypeStruct((16, COLS), BF),
            jax.ShapeDtypeStruct((LOCAL, COLS), BF),
        ),
        in_specs=[
            block,
            block,
            pl.BlockSpec((wide, RANK), lambda i: (i, 0)),
            pl.BlockSpec((2 * LOCAL + 16, RANK), lambda i: (0, 0)),
        ],
        out_specs=(block, pl.BlockSpec((16, wide), lambda i: (0, i)), block),
        compiler_params=pltpu.CompilerParams(vmem_limit_bytes=40 << 20),
        name="apply",
    )(momentum, gradient, zt, lhs)


def local(momentum, gradient, basis):
    zt, lhs = gather_call(momentum, gradient, basis)
    return apply_call(momentum, gradient, zt, lhs)


def solution(mesh):
    return jax.shard_map(
        local,
        mesh=mesh,
        in_specs=(P("rows", "cols"), P("rows", "cols"), P("rows", "cols")),
        out_specs=(P("rows", "cols"), P("rows", "cols"), P("rows", "cols")),
        check_vma=False,
    )
```

```python
import functools
import math

import jax
import jax.numpy as jnp
from jax import lax
from jax.experimental import pallas as pl
from jax.experimental.pallas import tpu as pltpu
from jax.sharding import PartitionSpec as P

ROWS = 12288
WIDTH = 26624
RANK = 512
MESH = pl.DeviceIdType.MESH
BF = jnp.bfloat16
F32 = jnp.float32

LOCAL = 384
COLS = 6656
HALF = 3328
PART = 1664
SEG = 832
SUB = 208
B = 128
N_SEMS = 224


def mod4(v):
    return lax.rem(v + 4, 4)


def rows_at(start, size, unit=16):
    return pl.ds(pl.multiple_of(start, unit), size)


def dotp(a, b, dims):
    return lax.dot_general(
        a, b, (dims, ((), ())), precision=lax.Precision.HIGHEST, preferred_element_type=F32
    )


def dotb(a, b, dims):
    return lax.dot_general(a, b, (dims, ((), ())), preferred_element_type=F32)


def split(a):
    hi = a.astype(BF)
    return hi, (a - hi.astype(F32)).astype(BF)


def tree(terms):
    while len(terms) > 1:
        terms = [a + b for a, b in zip(terms[::2], terms[1::2])]
    return terms[0]


def sweep(w_ref, t, hook):
    sub = lax.broadcasted_iota(jnp.int32, (8, B), 0)
    lane = lax.broadcasted_iota(jnp.int32, (8, B), 1)
    panels = B // 8
    for p in range(panels):
        top = t[:8]
        cols = jnp.stack(
            [jnp.broadcast_to(top[:, 8 * p + j : 8 * p + j + 1], (8, B)) for j in range(8)]
        )
        for j in range(0, 8, 2):
            d0 = jnp.broadcast_to(cols[j, j : j + 1, :], (8, B))
            off = jnp.broadcast_to(cols[j, j + 1 : j + 2, :], (8, B))
            d1 = jnp.broadcast_to(cols[j + 1, j + 1 : j + 2, :], (8, B))
            r0 = lax.rsqrt(d0)
            r1 = lax.rsqrt(d0 * d1 - off * off) * (d0 * r0)
            low = off * r0
            below = sub > j + 1
            m0 = jnp.where(below, cols[j] * r0, 0.0)
            m1 = jnp.where(below, (cols[j + 1] - m0 * low) * r1, 0.0)
            c0 = jnp.where(sub >= j, jnp.where(sub == j, 1.0, 0.0), cols[j])
            c1 = jnp.where(sub >= j, jnp.where(sub == j + 1, 1.0, 0.0), cols[j + 1])
            parts = [cols[:j]] if j else []
            parts += [c0[None], c1[None]]
            if j < 6:
                parts.append(cols[j + 2 :])
            cols = jnp.concatenate(parts, axis=0)
            s0 = cols[:, j : j + 1, :] * r0[None]
            s1 = (cols[:, j + 1 : j + 2, :] - low[None] * s0) * r1[None]
            rest = cols - m0[None] * s0 - m1[None] * s1
            cols = jnp.where((sub == j)[None], s0, jnp.where((sub == j + 1)[None], s1, rest))
        tri = [jnp.where(sub >= k, cols[k], 0.0) for k in range(8)]
        inside = (lane >= 8 * p) & (lane < 8 * p + 8)
        eye = jnp.where(inside, jnp.where(lane - 8 * p == sub, 1.0, 0.0), top)
        new = tree([tri[k] * eye[k : k + 1] for k in range(8)])
        w_ref[8 * p : 8 * p + 8, :] = jnp.where(lane <= sub + 8 * p, new, 0.0)
        if p < panels - 1:
            rest = t[8:]
            lanes = lax.broadcasted_iota(jnp.int32, rest.shape, 1)
            t = jnp.where((lanes >= 8 * p) & (lanes < 8 * p + 8), 0.0, rest)
            ys = [jnp.sum(tri[k] * new, axis=0, keepdims=True) for k in range(8)]
            t = t - tree([rest[:, 8 * p + k : 8 * p + k + 1] * ys[k] for k in range(8)])
        if p % 2 == 1:
            hook(p // 2)


def chol_inv(t_ref, w_ref, hook):
    lanes = lax.broadcasted_iota(jnp.int32, (B, RANK), 1)
    subs = lax.broadcasted_iota(jnp.int32, (B, RANK), 0)

    def block(k, carry):
        base = pl.multiple_of(k * B, B)
        rows = pl.ds(base, B)
        sweep(w_ref, t_ref[rows, rows], functools.partial(hook, k))
        own = (lanes >= base) & (lanes < base + B)
        mine = jnp.where(own, jnp.where(lanes - base == subs, 1.0, 0.0), t_ref[rows, :])
        new = dotp(w_ref[...], mine, ((1,), (0,)))
        t_ref[rows, :] = new

        def below(i, c):
            at = pl.ds(pl.multiple_of(i * B, B), B)
            t_ref[at, :] = jnp.where(own, 0.0, t_ref[at, :]) - dotp(
                t_ref[rows, at], new, ((0,), (0,))
            )
            return c

        lax.fori_loop(k + 1, RANK // B, below, 0)
        return carry

    lax.fori_loop(0, RANK // B, block, 0)


def gather_kernel(
    m_hbm, g_hbm, basis_hbm, buf_ref, zt_ref, lhs_ref,
    mbuf, gbuf, side, buf2t, bas, psum, pleft, psend, precv, chip_left, yr, left2,
    gs, gr, gram, tmat, wmat, zp, zown, zl, zrh, zrf, zr2, nr1, nr2,
    load_sem, send_sem, recv_sem,
):
    r = lax.axis_index("rows")
    y = lax.axis_index("cols")
    c = lax.rem(r, 2)
    z = lax.rem(lax.div(r, 2), 4)
    x = lax.div(r, 8)
    p1 = x * (1 - c) + z * c
    p2 = z * (1 - c) + x * c

    def chip(a, b):
        return a * (4 - 3 * c) + b * (1 + 3 * c)

    def device(a, b):
        return 2 * chip(a, b) + c

    sib = (r + 1 - 2 * c, y)
    a1p = (device(mod4(p1 + 1), p2), y)
    a1m = (device(mod4(p1 - 1), p2), y)
    a2p = (device(p1, mod4(p2 + 1)), y)
    a2m = (device(p1, mod4(p2 - 1)), y)
    plane = [(dx, dz) for dx in range(4) for dz in range(4) if dx or dz]

    def peer(dx, dz):
        return (mod4(x + dx) * 8 + mod4(z + dz) * 2 + c, y)

    def source_chip(dx, dz):
        return mod4(x - dx) * 4 + mod4(z - dz)

    group = [(dy, dc) for dy in range(4) for dc in range(2) if dy or dc]

    def member(dy, dc):
        return (r + dc * (1 - 2 * c), mod4(y + dy))

    count = [0]
    sent = []

    def plan(src, dst, to, landing):
        i = count[0]
        count[0] += 1

        def copy(s, d):
            return pltpu.make_async_remote_copy(
                s, d, send_sem.at[i], recv_sem.at[i], device_id=to, device_id_type=MESH
            )

        def start():
            copy(src, dst).start()
            sent.append(lambda: copy(src, dst).wait_send())

        return start, lambda: copy(landing, landing).wait_recv()

    def send(src, dst, to, landing):
        start, wait = plan(src, dst, to, landing)
        start()
        return wait

    def columns(core, part):
        return pl.ds(pl.multiple_of(core * HALF + part * PART, 128), PART)

    order = [(1 - c, 0), (1 - c, 1), (c, 0), (c, 1)]

    def load(n):
        at = columns(*order[n])
        return [
            pltpu.make_async_copy(m_hbm.at[:, at], mbuf.at[n % 2], load_sem.at[2 * n]),
            pltpu.make_async_copy(g_hbm.at[:, at], gbuf.at[n % 2], load_sem.at[2 * n + 1]),
        ]

    loads = [load(n) for n in range(4)]
    for n in range(2):
        for copy in loads[n]:
            copy.start()
    own_rows = rows_at(r * 16, 16)
    parts = [pl.ds(0, PART), pl.ds(PART, PART)]
    own_basis = [
        pltpu.make_async_copy(
            basis_hbm.at[:, columns(c, n)], bas.at[own_rows, parts[n]], load_sem.at[8 + n]
        )
        for n in range(2)
    ]
    for copy in own_basis:
        copy.start()

    barrier = pltpu.get_barrier_semaphore()
    others = [sib, a1p, a1m, a2p, a2m] + [(r, mod4(y + d)) for d in (1, 2, 3)]
    for to in others:
        pl.semaphore_signal(barrier, inc=1, device_id=to, device_id_type=MESH)
    pl.semaphore_wait(barrier, len(others))

    sib_ranks = rows_at((r + 1 - 2 * c) * 16, 16)
    got = [
        send(
            basis_hbm.at[:, columns(1 - c, n)],
            bas.at[own_rows, parts[n]],
            sib,
            bas.at[sib_ranks, parts[n]],
        )
        for n in range(2)
    ]

    def piece(a, b, n):
        return bas.at[rows_at(chip(a, b) * 32, 32), parts[n]]

    def half_piece(a, b, n, h):
        return bas.at[rows_at(chip(a, b) * 32 + 16 * h, 16), parts[n]]

    def at1(d):
        return mod4(p1 + d)

    def at2(d):
        return mod4(p2 + d)

    first = []
    for n in range(2):
        own_basis[n].wait()
        got[n]()
        mine = piece(p1, p2, n)
        first.append(
            (
                send(mine, mine, a1p, piece(at1(-1), p2, n)),
                send(mine, mine, a1m, piece(at1(1), p2, n)),
            )
        )

    def both2(a, n):
        ref = piece(a, p2, n)
        return (
            send(ref, ref, a2p, piece(a, at2(-1), n)),
            send(ref, ref, a2m, piece(a, at2(1), n)),
        )

    second = [[both2(p1, n)] for n in range(2)]

    def add_loaded(n):
        for copy in loads[n]:
            copy.wait()

        def step(i, carry):
            at = rows_at(i * 16, 16)
            total = mbuf[n % 2, at, :].astype(F32) + gbuf[n % 2, at, :].astype(F32)
            buf_ref[at, columns(*order[n])] = total.astype(BF)
            return carry

        lax.fori_loop(0, LOCAL // 16, step, 0)
        if n < 2:
            for copy in loads[n + 2]:
                copy.start()

    my_rows = rows_at(c * LOCAL, LOCAL, 128)
    sib_rows = rows_at((1 - c) * LOCAL, LOCAL, 128)

    def send_buffer(n):
        return send(
            buf_ref.at[:, columns(1 - c, n)], side.at[:, parts[n]], sib, side.at[:, parts[n]]
        )

    def turn(n, mine):
        def step(i, carry):
            at = rows_at(n * PART + i * 128, 128, 128)
            if mine:
                from_at = rows_at(c * HALF + n * PART + i * 128, 128, 128)
                buf2t[at, my_rows] = buf_ref[:, from_at].T
            else:
                buf2t[at, sib_rows] = side[:, at].T
            return carry

        lax.fori_loop(0, PART // 128, step, 0)

    add_loaded(0)
    swapped = [send_buffer(0)]
    opposite1 = []
    for n in range(2):
        from_m, from_p = first[n]
        from_m()
        ref = half_piece(at1(-1), p2, n, 0)
        opp0 = send(ref, ref, a1p, half_piece(at1(2), p2, n, 0))
        second[n].append(both2(at1(-1), n))
        from_p()
        ref = half_piece(at1(1), p2, n, 1)
        opp1 = send(ref, ref, a1m, half_piece(at1(2), p2, n, 1))
        second[n].append(both2(at1(1), n))
        opposite1.append((opp0, opp1))
    add_loaded(1)
    swapped.append(send_buffer(1))
    for n in range(2):
        for wait in opposite1[n]:
            wait()
        second[n].append(both2(at1(2), n))
    add_loaded(2)
    last = [[], []]
    offsets = (0, -1, 1, 2)

    def forward2(n, q):
        a = at1(offsets[q])
        from_m, from_p = second[n][q]
        from_m()
        ref = half_piece(a, at2(-1), n, 0)
        last[n].append(send(ref, ref, a2p, half_piece(a, at2(2), n, 0)))
        from_p()
        ref = half_piece(a, at2(1), n, 1)
        last[n].append(send(ref, ref, a2m, half_piece(a, at2(2), n, 1)))

    forward2(0, 0)
    forward2(0, 1)
    add_loaded(3)
    forward2(0, 2)
    forward2(0, 3)
    forward2(1, 0)
    turn(0, True)
    forward2(1, 1)
    turn(1, True)
    swapped[0]()
    turn(0, False)
    forward2(1, 2)
    swapped[1]()
    turn(1, False)
    forward2(1, 3)

    ranks = [pl.ds(0, 256), pl.ds(256, 256)]

    def left_part(mine, n, s):
        rows = buf_ref[:, columns(c, n)] if mine else side[:, parts[n]]
        return dotb(rows, bas[ranks[s], parts[n]], ((1,), (1,)))

    for wait in last[0]:
        wait()
    for s in range(2):
        psum[s] = left_part(False, 0, s)
        pleft[s] = left_part(True, 0, s)
    for wait in last[1]:
        wait()
    paired = []
    for s in range(2):
        psend[s] = (psum[s] + left_part(False, 1, s)).astype(BF)
        paired.append(send(psend.at[s], precv.at[s], sib, precv.at[s]))
        pleft[s] = pleft[s] + left_part(True, 1, s)

    def along_y(d):
        return (r, mod4(y + d))

    def left_rows(core, d):
        return rows_at(core * LOCAL + mod4(y + d) * 96, 96)

    summed = []
    for s in range(2):
        paired[s]()
        total = pleft[s] + precv[s].astype(F32)
        pleft[s] = total
        chip_left[s] = total.astype(BF)
        summed.append(
            [
                send(
                    chip_left.at[s, rows_at(mod4(y + d) * 96, 96)],
                    yr.at[s, d - 1],
                    along_y(d),
                    yr.at[s, d - 1],
                )
                for d in (2, 1, 3)
            ]
        )
    spread, pairs = [], []
    for s in range(2):
        for wait in summed[s]:
            wait()
        total = pleft[s, rows_at(y * 96, 96), :]
        for d in range(3):
            total = total + yr[s, d].astype(F32)
        left2[s, left_rows(c, 0), :] = total.astype(BF)
        ref = left2.at[s, left_rows(c, 0)]
        spread.append(
            {d: send(ref, ref, along_y(d), left2.at[s, left_rows(c, -d)]) for d in (2, 1, 3)}
        )
        pairs.append([send(ref, ref, sib, left2.at[s, left_rows(1 - c, 0)])])

    def left_done(s):
        for d in (1, 3, 2):
            spread[s][d]()
            ref = left2.at[s, left_rows(c, -d)]
            pairs[s].append(send(ref, ref, sib, left2.at[s, left_rows(1 - c, -d)]))
        for wait in pairs[s]:
            wait()

    def z_value(d, h, s):
        at = rows_at(mod4(p1 + d) * SEG + (SEG // 2) * h, SEG // 2)
        return dotb(buf2t[at, :], left2[s], ((1,), (0,)))

    ways = (a1p, a1m)
    z_half = [[], []]
    z_full = [[], []]

    def z_first(s):
        for w in range(2):
            zp[s, 2, w] = z_value(2, w, s).astype(BF)
            z_half[s].append(send(zp.at[s, 2, w], zrh.at[s, w], ways[w], zrh.at[s, w]))

    def z_middle(s):
        for w, (d, h) in enumerate(((1, 1), (3, 0))):
            zp[s, d, h] = z_value(d, h, s).astype(BF)
            z_full[s].append(send(zp.at[s, d, h], zrf.at[s, w, h], ways[w], zrf.at[s, w, h]))

    def z_prepare(s):
        for w, (d, h) in enumerate(((1, 0), (3, 1))):
            zl[s, w] = z_value(d, h, s)

    def z_add(s):
        for w, (d, h) in enumerate(((1, 0), (3, 1))):
            z_half[s][w]()
            zp[s, d, h] = (zl[s, w] + zrh[s, w].astype(F32)).astype(BF)
            z_full[s].append(send(zp.at[s, d, h], zrf.at[s, w, h], ways[w], zrf.at[s, w, h]))

    def z_own(s):
        for h in range(2):
            zown[s, h] = z_value(0, h, s)

    left_done(0)
    z_first(0)
    left_done(1)

    blocks = [(i, j) for i in range(4) for j in range(i, 4)]

    def left_block(i):
        return left2[i // 2, :, 128 * (i % 2) : 128 * (i % 2) + 128]

    for b, (i, j) in enumerate(blocks):
        gs[b] = dotb(left_block(i), left_block(j), ((0,), (0,)))

    def tile(j):
        return pl.ds(lax.rem(j, 2) * 5, 5), rows_at(c * 64 + lax.div(j, 2) * 8, 8, 8)

    gram_in = []
    for e, (dx, dz) in enumerate(plane):
        to = tile(mod4(x + dx) * 4 + mod4(z + dz))
        gram_in.append(send(gs.at[to], gr.at[e], peer(dx, dz), gr.at[e]))
    z_first(1)
    z_middle(0)
    for wait in gram_in:
        wait()
    mine = tile(x * 4 + z)
    gram[mine] = gs[mine] + tree([gr[e] for e in range(15)] + [jnp.zeros((5, 8, B), F32)])
    gathered = []
    for dx, dz in plane:
        ref = gram.at[mine]
        gathered.append(send(ref, ref, peer(dx, dz), gram.at[tile(source_chip(dx, dz))]))
    z_middle(1)
    z_prepare(0)
    z_add(0)
    z_prepare(1)
    z_add(1)
    z_own(0)
    z_own(1)
    for wait in gathered:
        wait()
    ref = gram.at[:, rows_at(c * 64, 64)]
    send(ref, ref, sib, gram.at[:, rows_at((1 - c) * 64, 64)])()

    on = lax.broadcasted_iota(jnp.int32, (B, B), 0) == lax.broadcasted_iota(jnp.int32, (B, B), 1)
    across, down = [], []
    for i in range(4):
        diag = jnp.where(on, gram[blocks.index((i, i))], 0.0)
        across.append(lax.rsqrt(jnp.sum(diag, axis=0, keepdims=True)))
        down.append(lax.rsqrt(jnp.sum(diag, axis=1, keepdims=True)))
    for i in range(4):
        for j in range(4):
            if j < i:
                block = jnp.zeros((B, B), F32)
            else:
                block = gram[blocks.index((i, j))] * down[i] * across[j]
            tmat[B * i : B * i + B, B * j : B * j + B] = block

    def sub_rows(a, b):
        return rows_at(c * HALF + a * SEG + b * SUB, SUB)

    def sub_half(a, b, h):
        return rows_at(c * HALF + a * SEG + b * SUB + 112 * h, 112 - 16 * h)

    def to_sib(a, d, s):
        ref = zt_ref.at[sub_rows(at1(a), at2(d)), ranks[s]]
        start = (1 - c) * HALF + at2(a) * SEG + at1(d) * SUB
        return plan(ref, ref, sib, zt_ref.at[rows_at(start, SUB), ranks[s]])

    def part(b, s):
        return zp.at[s, 0, lax.div(b, 2), rows_at(lax.rem(b, 2) * SUB, SUB)]

    z2, z3, z4, z5, zs = {}, {}, {}, {}, {}
    for s in range(2):

        def sub(a, b, s=s):
            return zt_ref.at[sub_rows(a, b), ranks[s]]

        def half(a, b, h, s=s):
            return zt_ref.at[sub_half(a, b, h), ranks[s]]

        own = sub(p1, p2)
        for d in (2, 1, 3):
            to = (device(p1, at2(d)), y)
            z2[s, d] = plan(part(at2(d), s), zr2.at[s, d - 1], to, zr2.at[s, d - 1])
            z3[s, d] = plan(own, own, to, sub(p1, at2(-d)))
        for d in range(4):
            b = at2(d)
            ref = sub(p1, b)
            z4[s, d] = (
                plan(ref, ref, a1p, sub(at1(-1), b)),
                plan(ref, ref, a1m, sub(at1(1), b)),
            )
            ref, ref1 = half(at1(-1), b, 0), half(at1(1), b, 1)
            z5[s, d] = (
                plan(ref, ref, a1p, half(at1(2), b, 0)),
                plan(ref1, ref1, a1m, half(at1(2), b, 1)),
            )
            for a in range(4):
                zs[s, a, d] = to_sib(a, d, s)

    def z_sum1(s):
        for wait in z_full[s]:
            wait()

        def step(i, carry):
            h, at = lax.div(i, 2), rows_at(lax.rem(i, 2) * SUB, SUB)
            total = zown[s, h, at, :] + zrf[s, 0, h, at, :].astype(F32)
            total = total + zrf[s, 1, h, at, :].astype(F32)
            zp[s, 0, h, at, :] = total.astype(BF)
            return carry

        lax.fori_loop(0, 4, step, 0)
        for d in (2, 1, 3):
            z2[s, d][0]()

    def z_out(d, s):
        z4[s, d][0][0]()
        z4[s, d][1][0]()
        zs[s, 0, d][0]()

    def z_sum2(s):
        for d in (1, 3, 2):
            z2[s, d][1]()
        total = zp[s, 0, lax.div(p2, 2), rows_at(lax.rem(p2, 2) * SUB, SUB), :].astype(F32)
        for d in range(3):
            total = total + zr2[s, d].astype(F32)
        zt_ref[sub_rows(p1, p2), ranks[s]] = total.astype(BF)
        for d in (2, 1, 3):
            z3[s, d][0]()
        z_out(0, s)

    def z_gather2(d, s):
        z3[s, d][1]()
        z_out((4 - d) % 4, s)

    def z_forward(d, s):
        (_, from_m), (_, from_p) = z4[s, d]
        from_m()
        z5[s, d][0][0]()
        zs[s, 3, d][0]()
        from_p()
        z5[s, d][1][0]()
        zs[s, 1, d][0]()

    def z_last(d, s):
        for _, wait in z5[s, d]:
            wait()
        zs[s, 2, d][0]()

    steps = {
        (0, 5): lambda: z_sum1(0),
        (1, 1): lambda: z_sum1(1),
        (2, 0): lambda: z_sum2(0),
        (2, 6): lambda: z_sum2(1),
        (3, 0): lambda: z_forward(0, 0),
        (3, 2): lambda: z_gather2(1, 0),
        (3, 3): lambda: z_gather2(3, 0),
        (3, 4): lambda: z_gather2(2, 0),
        (3, 5): lambda: z_forward(0, 1),
        (3, 7): lambda: z_gather2(1, 1),
    }

    def hook(k, part):
        for (at, which), step in steps.items():
            if which == part:
                pl.when(k == at)(step)

    chol_inv(tmat, wmat, hook)
    ri = lax.broadcasted_iota(jnp.int32, (RANK, RANK), 0)
    ci = lax.broadcasted_iota(jnp.int32, (RANK, RANK), 1)
    tmat[...] = jnp.where(ci <= ri, tmat[...], 0.0) * jnp.concatenate(across, axis=1)
    w_hi, w_lo = split(tmat[...])

    shard = zt_ref[sub_rows(p1, p2), :]
    right = dotb(shard, w_hi, ((1,), (1,))) + dotb(shard, w_lo, ((1,), (1,)))
    squares = jnp.sum(right * right, axis=0, keepdims=True)
    rows = [squares[:, B * i : B * i + B] for i in range(4)] + [jnp.zeros((4, B), F32)]
    nr1[0] = jnp.concatenate(rows, axis=0)
    norm_in = [
        send(nr1.at[0], nr1.at[e + 1], peer(dx, dz), nr1.at[e + 1])
        for e, (dx, dz) in enumerate(plane)
    ]
    z_gather2(3, 1)
    z_gather2(2, 1)
    own_left = jnp.concatenate([left2[0, my_rows, :], left2[1, my_rows, :]], axis=1)
    ortho = (dotb(own_left, w_hi, ((1,), (1,))) + dotb(own_left, w_lo, ((1,), (1,)))).astype(BF)
    z_forward(3, 0)
    z_forward(1, 0)
    lhs_ref[0:LOCAL, :] = (
        dotb(ortho, w_hi, ((1,), (0,))) + dotb(ortho, w_lo, ((1,), (0,)))
    ).astype(BF)
    z_forward(2, 0)
    z_last(0, 0)
    for wait in norm_in:
        wait()
    nr2[0] = tree([nr1[e] for e in range(16)])
    norm_in = [
        send(nr2.at[0], nr2.at[f + 1], member(dy, dc), nr2.at[f + 1])
        for f, (dy, dc) in enumerate(group)
    ]
    z_forward(3, 1)
    z_forward(1, 1)
    z_forward(2, 1)
    z_last(0, 1)
    for wait in norm_in:
        wait()
    total = tree([nr2[f] for f in range(8)])
    total = jnp.concatenate([total[i : i + 1] for i in range(4)], axis=1)
    scale = lax.rsqrt(total + 1e-06)
    sub16 = lax.broadcasted_iota(jnp.int32, (16, RANK), 0)
    lane16 = lax.broadcasted_iota(jnp.int32, (16, RANK), 1)
    pick = jnp.where(lane16 == sub16 + r * 16, scale, 0.0)
    o_hi, o_lo = split(jnp.concatenate([ortho.astype(F32) * scale, pick], axis=0))
    lhs_ref[LOCAL : 2 * LOCAL + 16, :] = (
        dotb(o_hi, w_hi, ((1,), (0,)))
        + (dotb(o_hi, w_lo, ((1,), (0,))) + dotb(o_lo, w_hi, ((1,), (0,))))
    ).astype(BF)
    for s in range(2):
        for d in (3, 1, 2):
            z_last(d, s)
    for _, wait in zs.values():
        wait()
    for wait in sent:
        wait()


def gather_call(momentum, gradient, basis):
    anyspace = pl.BlockSpec(memory_space=pl.ANY)
    vmem = pl.BlockSpec(memory_space=pltpu.VMEM)
    scratch = [
        ((2, LOCAL, PART), BF),
        ((2, LOCAL, PART), BF),
        ((LOCAL, HALF), BF),
        ((HALF, 2 * LOCAL), BF),
        ((RANK, HALF), BF),
        ((2, LOCAL, 256), F32),
        ((2, LOCAL, 256), F32),
        ((2, LOCAL, 256), BF),
        ((2, LOCAL, 256), BF),
        ((2, LOCAL, 256), BF),
        ((2, 3, 96, 256), BF),
        ((2, 2 * LOCAL, 256), BF),
        ((10, B, B), F32),
        ((15, 5, 8, B), F32),
        ((10, B, B), F32),
        ((RANK, RANK), F32),
        ((B, B), F32),
        ((2, 4, 2, SEG // 2, 256), BF),
        ((2, 2, SEG // 2, 256), F32),
        ((2, 2, SEG // 2, 256), F32),
        ((2, 2, SEG // 2, 256), BF),
        ((2, 2, 2, SEG // 2, 256), BF),
        ((2, 3, SUB, 256), BF),
        ((16, 8, B), F32),
        ((8, 8, B), F32),
    ]
    return pl.pallas_call(
        gather_kernel,
        out_shape=(
            pltpu.VMEM((LOCAL, COLS), BF),
            pltpu.VMEM((COLS, RANK), BF),
            pltpu.VMEM((2 * LOCAL + 16, RANK), BF),
        ),
        in_specs=[anyspace] * 3,
        out_specs=(vmem,) * 3,
        scratch_shapes=[pltpu.VMEM(s, t) for s, t in scratch]
        + [
            pltpu.SemaphoreType.DMA((10,)),
            pltpu.SemaphoreType.DMA((N_SEMS,)),
            pltpu.SemaphoreType.DMA((N_SEMS,)),
        ],
        compiler_params=pltpu.CompilerParams(
            collective_id=0, has_side_effects=True, vmem_limit_bytes=44 << 20
        ),
        name="project",
    )(momentum, gradient, basis)


def apply_kernel(buf_ref, zt_ref, lhs_ref, mom_ref, bas_ref, upd_ref):
    wide = mom_ref.shape[1]
    cols = rows_at(pl.program_id(0) * wide, wide, 128)
    prod = dotb(lhs_ref[...], zt_ref[cols, :], ((1,), (1,)))
    mom_ref[...] = (buf_ref[:, cols].astype(F32) - 0.2 * prod[:LOCAL]).astype(BF)
    factor = math.sqrt(ROWS * WIDTH / RANK)
    upd_ref[...] = (factor * prod[LOCAL : 2 * LOCAL]).astype(BF)
    bas_ref[...] = prod[2 * LOCAL :].astype(BF)


def apply_call(buf, zt, lhs):
    wide = 1664
    block = pl.BlockSpec((LOCAL, wide), lambda i: (0, i))
    held = [pltpu.with_memory_space_constraint(v, pltpu.VMEM) for v in (buf, zt, lhs)]
    return pl.pallas_call(
        apply_kernel,
        grid=(COLS // wide,),
        out_shape=(
            jax.ShapeDtypeStruct((LOCAL, COLS), BF),
            jax.ShapeDtypeStruct((16, COLS), BF),
            jax.ShapeDtypeStruct((LOCAL, COLS), BF),
        ),
        in_specs=[pl.BlockSpec(memory_space=pltpu.VMEM)] * 3,
        out_specs=(block, pl.BlockSpec((16, wide), lambda i: (0, i)), block),
        compiler_params=pltpu.CompilerParams(vmem_limit_bytes=24 << 20),
        name="apply",
    )(*held)


def local(momentum, gradient, basis):
    return apply_call(*gather_call(momentum, gradient, basis))


def solution(mesh):
    return jax.shard_map(
        local,
        mesh=mesh,
        in_specs=(P("rows", "cols"), P("rows", "cols"), P("rows", "cols")),
        out_specs=(P("rows", "cols"), P("rows", "cols"), P("rows", "cols")),
        check_vma=False,
    )
```

```python
import functools
import math

import jax
import jax.numpy as jnp
from jax import lax
from jax.experimental import pallas as pl
from jax.experimental.pallas import tpu as pltpu
from jax.sharding import PartitionSpec as P

ROWS = 12288
WIDTH = 26624
RANK = 512
MESH = pl.DeviceIdType.MESH
BF = jnp.bfloat16
F32 = jnp.float32

LOCAL = 384
COLS = 6656
HALF = 3328
PART = 1664
SEG = 832
SUB = 208
B = 128
N_SEMS = 224


def mod4(v):
    return lax.rem(v + 4, 4)


def rows_at(start, size, unit=16):
    return pl.ds(pl.multiple_of(start, unit), size)


def dotp(a, b, dims):
    return lax.dot_general(
        a, b, (dims, ((), ())), precision=lax.Precision.HIGHEST, preferred_element_type=F32
    )


def dotb(a, b, dims):
    return lax.dot_general(a, b, (dims, ((), ())), preferred_element_type=F32)


def split(a):
    hi = a.astype(BF)
    return hi, (a - hi.astype(F32)).astype(BF)


def tree(terms):
    while len(terms) > 1:
        terms = [a + b for a, b in zip(terms[::2], terms[1::2])]
    return terms[0]


def sweep(w_ref, t, hook):
    sub = lax.broadcasted_iota(jnp.int32, (8, B), 0)
    lane = lax.broadcasted_iota(jnp.int32, (8, B), 1)
    panels = B // 8
    for p in range(panels):
        top = t[:8]
        cols = jnp.stack(
            [jnp.broadcast_to(top[:, 8 * p + j : 8 * p + j + 1], (8, B)) for j in range(8)]
        )
        for j in range(0, 8, 2):
            d0 = jnp.broadcast_to(cols[j, j : j + 1, :], (8, B))
            off = jnp.broadcast_to(cols[j, j + 1 : j + 2, :], (8, B))
            d1 = jnp.broadcast_to(cols[j + 1, j + 1 : j + 2, :], (8, B))
            r0 = lax.rsqrt(d0)
            r1 = lax.rsqrt(d0 * d1 - off * off) * (d0 * r0)
            low = off * r0
            below = sub > j + 1
            m0 = jnp.where(below, cols[j] * r0, 0.0)
            m1 = jnp.where(below, (cols[j + 1] - m0 * low) * r1, 0.0)
            c0 = jnp.where(sub >= j, jnp.where(sub == j, 1.0, 0.0), cols[j])
            c1 = jnp.where(sub >= j, jnp.where(sub == j + 1, 1.0, 0.0), cols[j + 1])
            parts = [cols[:j]] if j else []
            parts += [c0[None], c1[None]]
            if j < 6:
                parts.append(cols[j + 2 :])
            cols = jnp.concatenate(parts, axis=0)
            s0 = cols[:, j : j + 1, :] * r0[None]
            s1 = (cols[:, j + 1 : j + 2, :] - low[None] * s0) * r1[None]
            rest = cols - m0[None] * s0 - m1[None] * s1
            cols = jnp.where((sub == j)[None], s0, jnp.where((sub == j + 1)[None], s1, rest))
        tri = [jnp.where(sub >= k, cols[k], 0.0) for k in range(8)]
        inside = (lane >= 8 * p) & (lane < 8 * p + 8)
        eye = jnp.where(inside, jnp.where(lane - 8 * p == sub, 1.0, 0.0), top)
        new = tree([tri[k] * eye[k : k + 1] for k in range(8)])
        w_ref[8 * p : 8 * p + 8, :] = jnp.where(lane <= sub + 8 * p, new, 0.0)
        if p < panels - 1:
            rest = t[8:]
            lanes = lax.broadcasted_iota(jnp.int32, rest.shape, 1)
            t = jnp.where((lanes >= 8 * p) & (lanes < 8 * p + 8), 0.0, rest)
            ys = [jnp.sum(tri[k] * new, axis=0, keepdims=True) for k in range(8)]
            t = t - tree([rest[:, 8 * p + k : 8 * p + k + 1] * ys[k] for k in range(8)])
        if p % 2 == 1:
            hook(p // 2)


def chol_inv(t_ref, w_ref, hook):
    lanes = lax.broadcasted_iota(jnp.int32, (B, RANK), 1)
    subs = lax.broadcasted_iota(jnp.int32, (B, RANK), 0)

    def block(k, carry):
        base = pl.multiple_of(k * B, B)
        rows = pl.ds(base, B)
        sweep(w_ref, t_ref[rows, rows], functools.partial(hook, k))
        own = (lanes >= base) & (lanes < base + B)
        mine = jnp.where(own, jnp.where(lanes - base == subs, 1.0, 0.0), t_ref[rows, :])
        new = dotp(w_ref[...], mine, ((1,), (0,)))
        t_ref[rows, :] = new

        def below(i, c):
            at = pl.ds(pl.multiple_of(i * B, B), B)
            t_ref[at, :] = jnp.where(own, 0.0, t_ref[at, :]) - dotp(
                t_ref[rows, at], new, ((0,), (0,))
            )
            return c

        lax.fori_loop(k + 1, RANK // B, below, 0)
        return carry

    lax.fori_loop(0, RANK // B, block, 0)


def gather_kernel(
    m_hbm, g_hbm, basis_hbm, buf_ref, zt_ref, lhs_ref,
    mbuf, gbuf, side, buf2t, bas, pleft, psend, precv, chip_left, yr, left2,
    gs, gr, gram, tmat, wmat, zp, zown, zl, zrh, zrf, zr2, nr1, nr2, onehot, ltrue, feed,
    load_sem, send_sem, recv_sem,
):
    r = lax.axis_index("rows")
    y = lax.axis_index("cols")
    c = lax.rem(r, 2)
    z = lax.rem(lax.div(r, 2), 4)
    x = lax.div(r, 8)
    p1 = x * (1 - c) + z * c
    p2 = z * (1 - c) + x * c

    def chip(a, b):
        return a * (4 - 3 * c) + b * (1 + 3 * c)

    def device(a, b):
        return 2 * chip(a, b) + c

    sib = (r + 1 - 2 * c, y)
    a1p = (device(mod4(p1 + 1), p2), y)
    a1m = (device(mod4(p1 - 1), p2), y)
    a2p = (device(p1, mod4(p2 + 1)), y)
    a2m = (device(p1, mod4(p2 - 1)), y)
    plane = [(dx, dz) for dx in range(4) for dz in range(4) if dx or dz]

    def peer(dx, dz):
        return (mod4(x + dx) * 8 + mod4(z + dz) * 2 + c, y)

    def source_chip(dx, dz):
        return mod4(x - dx) * 4 + mod4(z - dz)

    group = [(dy, dc) for dy in range(4) for dc in range(2) if dy or dc]

    def member(dy, dc):
        return (r + dc * (1 - 2 * c), mod4(y + dy))

    count = [0]
    sent = []

    def plan(src, dst, to, landing):
        i = count[0]
        count[0] += 1

        def copy(s, d):
            return pltpu.make_async_remote_copy(
                s, d, send_sem.at[i], recv_sem.at[i], device_id=to, device_id_type=MESH
            )

        def start():
            copy(src, dst).start()
            sent.append(lambda: copy(src, dst).wait_send())

        return start, lambda: copy(landing, landing).wait_recv()

    def send(src, dst, to, landing):
        start, wait = plan(src, dst, to, landing)
        start()
        return wait

    def columns(core, part):
        return pl.ds(pl.multiple_of(core * HALF + part * PART, 128), PART)

    order = [(1 - c, 0), (1 - c, 1), (c, 0), (c, 1)]

    def load(n):
        at = columns(*order[n])
        return [
            pltpu.make_async_copy(m_hbm.at[:, at], mbuf.at[n % 2], load_sem.at[2 * n]),
            pltpu.make_async_copy(g_hbm.at[:, at], gbuf.at[n % 2], load_sem.at[2 * n + 1]),
        ]

    loads = [load(n) for n in range(4)]
    for n in range(2):
        for copy in loads[n]:
            copy.start()
    parts = [pl.ds(0, PART), pl.ds(PART, PART)]

    def half_of(core):
        return pl.ds(pl.multiple_of(core * HALF, 128), HALF)

    def chip_rows(a, b):
        return rows_at(chip(a, b) * 16, 16)

    here = chip_rows(p1, p2)
    own_basis = pltpu.make_async_copy(
        basis_hbm.at[:, half_of(c)], bas.at[c, here], load_sem.at[8]
    )
    own_basis.start()

    barrier = pltpu.get_barrier_semaphore()
    others = [sib, a1p, a1m, a2p, a2m] + [(r, mod4(y + d)) for d in (1, 2, 3)]
    for to in others:
        pl.semaphore_signal(barrier, inc=1, device_id=to, device_id_type=MESH)
    pl.semaphore_wait(barrier, len(others))

    got = send(basis_hbm.at[:, half_of(1 - c)], bas.at[c, here], sib, bas.at[1 - c, here])

    def piece(a, b, n):
        return bas.at[n, chip_rows(a, b)]

    def half_piece(a, b, n, h):
        return bas.at[n, chip_rows(a, b), parts[h]]

    def at1(d):
        return mod4(p1 + d)

    def at2(d):
        return mod4(p2 + d)

    own_basis.wait()
    got()
    first = [None, None]
    second = [[], []]
    opposite1 = [None, None]

    def both2(d, n):
        a = at1(d)
        ref = piece(a, p2, n)
        second[n].append(
            (
                send(ref, ref, a2p, piece(a, at2(-1), n)),
                send(ref, ref, a2m, piece(a, at2(1), n)),
            )
        )

    def start(n):
        mine = piece(p1, p2, n)
        first[n] = (
            send(mine, mine, a1p, piece(at1(-1), p2, n)),
            send(mine, mine, a1m, piece(at1(1), p2, n)),
        )
        both2(0, n)

    def pass_on(n):
        from_m, from_p = first[n]
        from_m()
        ref = half_piece(at1(-1), p2, n, 0)
        opp0 = send(ref, ref, a1p, half_piece(at1(2), p2, n, 0))
        both2(-1, n)
        from_p()
        ref = half_piece(at1(1), p2, n, 1)
        opp1 = send(ref, ref, a1m, half_piece(at1(2), p2, n, 1))
        both2(1, n)
        opposite1[n] = (opp0, opp1)

    def opposite(n):
        for wait in opposite1[n]:
            wait()
        both2(2, n)

    start(0)

    def add_loaded(n):
        for copy in loads[n]:
            copy.wait()

        def step(i, carry):
            at = rows_at(i * 16, 16)
            total = mbuf[n % 2, at, :].astype(F32) + gbuf[n % 2, at, :].astype(F32)
            buf_ref[at, columns(*order[n])] = total.astype(BF)
            return carry

        lax.fori_loop(0, LOCAL // 16, step, 0)
        if n < 2:
            for copy in loads[n + 2]:
                copy.start()

    my_rows = rows_at(c * LOCAL, LOCAL, 128)
    sib_rows = rows_at((1 - c) * LOCAL, LOCAL, 128)

    def send_buffer(n):
        return send(
            buf_ref.at[:, columns(1 - c, n)], side.at[:, parts[n]], sib, side.at[:, parts[n]]
        )

    def turn(n, mine):
        def step(i, carry):
            at = rows_at(n * PART + i * 128, 128, 128)
            if mine:
                from_at = rows_at(c * HALF + n * PART + i * 128, 128, 128)
                buf2t[at, my_rows] = buf_ref[:, from_at].T
            else:
                buf2t[at, sib_rows] = side[:, at].T
            return carry

        lax.fori_loop(0, PART // 128, step, 0)

    last = [[], []]
    offsets = (0, -1, 1, 2)

    def forward2(n, q):
        a = at1(offsets[q])
        from_m, from_p = second[n][q]
        from_m()
        ref = half_piece(a, at2(-1), n, 0)
        last[n].append(send(ref, ref, a2p, half_piece(a, at2(2), n, 0)))
        from_p()
        ref = half_piece(a, at2(1), n, 1)
        last[n].append(send(ref, ref, a2m, half_piece(a, at2(2), n, 1)))

    ranks = [pl.ds(0, 256), pl.ds(256, 256)]

    def sub_rows(a, b):
        return rows_at(c * HALF + a * SEG + b * SUB, SUB)

    def sub_half(a, b, h):
        return rows_at(c * HALF + a * SEG + b * SUB + 112 * h, 112 - 16 * h)

    def to_sib(a, d, s):
        ref = zt_ref.at[sub_rows(at1(a), at2(d)), ranks[s]]
        start = (1 - c) * HALF + at2(a) * SEG + at1(d) * SUB
        return plan(ref, ref, sib, zt_ref.at[rows_at(start, SUB), ranks[s]])

    def part(b, s):
        return zp.at[s, 0, lax.div(b, 2), rows_at(lax.rem(b, 2) * SUB, SUB)]

    z2, z3, z4, z5, zs = {}, {}, {}, {}, {}
    for s in range(2):

        def sub(a, b, s=s):
            return zt_ref.at[sub_rows(a, b), ranks[s]]

        def half(a, b, h, s=s):
            return zt_ref.at[sub_half(a, b, h), ranks[s]]

        own = sub(p1, p2)
        for d in (2, 1, 3):
            to = (device(p1, at2(d)), y)
            z2[s, d] = plan(part(at2(d), s), zr2.at[s, d - 1], to, zr2.at[s, d - 1])
            z3[s, d] = plan(own, own, to, sub(p1, at2(-d)))
        for d in range(4):
            b = at2(d)
            ref = sub(p1, b)
            z4[s, d] = (
                plan(ref, ref, a1p, sub(at1(-1), b)),
                plan(ref, ref, a1m, sub(at1(1), b)),
            )
            ref, ref1 = half(at1(-1), b, 0), half(at1(1), b, 1)
            z5[s, d] = (
                plan(ref, ref, a1p, half(at1(2), b, 0)),
                plan(ref1, ref1, a1m, half(at1(2), b, 1)),
            )
            for a in range(4):
                zs[s, a, d] = to_sib(a, d, s)

    def z_sum1(s):
        for wait in z_full[s]:
            wait()

        def step(i, carry):
            h, at = lax.div(i, 2), rows_at(lax.rem(i, 2) * SUB, SUB)
            total = zown[s, h, at, :] + zrf[s, 0, h, at, :].astype(F32)
            total = total + zrf[s, 1, h, at, :].astype(F32)
            zp[s, 0, h, at, :] = total.astype(BF)
            return carry

        lax.fori_loop(0, 4, step, 0)
        for d in (2, 1, 3):
            z2[s, d][0]()

    def z_out(d, s):
        z4[s, d][0][0]()
        z4[s, d][1][0]()
        zs[s, 0, d][0]()

    def z_sum2(s):
        for d in (1, 3, 2):
            z2[s, d][1]()
        total = zp[s, 0, lax.div(p2, 2), rows_at(lax.rem(p2, 2) * SUB, SUB), :].astype(F32)
        for d in range(3):
            total = total + zr2[s, d].astype(F32)
        zt_ref[sub_rows(p1, p2), ranks[s]] = total.astype(BF)
        for d in (2, 1, 3):
            z3[s, d][0]()
        z_out(0, s)

    def z_gather2(d, s):
        z3[s, d][1]()
        z_out((4 - d) % 4, s)

    def z_forward(d, s):
        (_, from_m), (_, from_p) = z4[s, d]
        from_m()
        z5[s, d][0][0]()
        zs[s, 3, d][0]()
        from_p()
        z5[s, d][1][0]()
        zs[s, 1, d][0]()

    def z_last(d, s):
        for _, wait in z5[s, d]:
            wait()
        zs[s, 2, d][0]()

    for n in range(2):
        k = lax.broadcasted_iota(jnp.int32, (256, RANK), 0)
        rank = lax.shift_right_logical(k, 4) * 32 + (k & 15) + 16 * n
        hit = lax.broadcasted_iota(jnp.int32, (256, RANK), 1) == rank
        onehot[n] = jnp.where(hit, 1.0, 0.0).astype(BF)

    paired, summed, spread, pairs = [], [], [], []

    def left_pair(s):
        for wait in last[s]:
            wait()
        psend[s] = dotb(side[...], bas[s], ((1,), (1,))).astype(BF)
        paired.append(send(psend.at[s], precv.at[s], sib, precv.at[s]))
        pleft[s] = dotb(buf_ref[:, half_of(c)], bas[s], ((1,), (1,)))

    def along_y(d):
        return (r, mod4(y + d))

    def left_rows(core, d):
        return rows_at(core * LOCAL + mod4(y + d) * 96, 96)

    def left_sum(s):
        paired[s]()
        total = pleft[s] + precv[s].astype(F32)
        pleft[s] = total
        chip_left[s] = total.astype(BF)
        summed.append(
            [
                send(
                    chip_left.at[s, rows_at(mod4(y + d) * 96, 96)],
                    yr.at[s, d - 1],
                    along_y(d),
                    yr.at[s, d - 1],
                )
                for d in (2, 1, 3)
            ]
        )

    def left_spread(s):
        for wait in summed[s]:
            wait()
        total = pleft[s, rows_at(y * 96, 96), :]
        for d in range(3):
            total = total + yr[s, d].astype(F32)
        left2[s, left_rows(c, 0), :] = total.astype(BF)
        ref = left2.at[s, left_rows(c, 0)]
        spread.append(
            {d: send(ref, ref, along_y(d), left2.at[s, left_rows(c, -d)]) for d in (2, 1, 3)}
        )
        pairs.append([send(ref, ref, sib, left2.at[s, left_rows(1 - c, 0)])])

    def left_done(s):
        for d in (1, 3, 2):
            spread[s][d]()
            ref = left2.at[s, left_rows(c, -d)]
            pairs[s].append(send(ref, ref, sib, left2.at[s, left_rows(1 - c, -d)]))
        for wait in pairs[s]:
            wait()

    def z_value(d, h, s):
        at = rows_at(mod4(p1 + d) * SEG + (SEG // 2) * h, SEG // 2)
        return dotb(buf2t[at, :], left2[s], ((1,), (0,)))

    ways = (a1p, a1m)
    z_half = [[], []]
    z_full = [[], []]

    def z_first(s):
        for w in range(2):
            zp[s, 2, w] = z_value(2, w, s).astype(BF)
            z_half[s].append(send(zp.at[s, 2, w], zrh.at[s, w], ways[w], zrh.at[s, w]))

    def z_middle(s):
        for w, (d, h) in enumerate(((1, 1), (3, 0))):
            zp[s, d, h] = z_value(d, h, s).astype(BF)
            z_full[s].append(send(zp.at[s, d, h], zrf.at[s, w, h], ways[w], zrf.at[s, w, h]))

    def z_prepare(s):
        for w, (d, h) in enumerate(((1, 0), (3, 1))):
            zl[s, w] = z_value(d, h, s)

    def z_add(s):
        for w, (d, h) in enumerate(((1, 0), (3, 1))):
            z_half[s][w]()
            zp[s, d, h] = (zl[s, w] + zrh[s, w].astype(F32)).astype(BF)
            z_full[s].append(send(zp.at[s, d, h], zrf.at[s, w, h], ways[w], zrf.at[s, w, h]))

    def z_own(s):
        for h in range(2):
            zown[s, h] = z_value(0, h, s)

    add_loaded(0)
    swapped = [send_buffer(0)]
    swap_sent = [sent.pop()]
    pass_on(0)
    start(1)
    add_loaded(1)
    swapped.append(send_buffer(1))
    swap_sent.append(sent.pop())
    opposite(0)
    add_loaded(2)
    forward2(0, 0)
    forward2(0, 1)
    forward2(0, 2)
    pass_on(1)
    add_loaded(3)
    forward2(0, 3)
    opposite(1)
    turn(0, True)
    turn(1, True)
    forward2(1, 0)
    for wait in swapped:
        wait()
    left_pair(0)
    forward2(1, 1)
    left_sum(0)
    forward2(1, 2)
    turn(0, False)
    turn(1, False)
    forward2(1, 3)
    left_spread(0)
    left_pair(1)
    left_sum(1)
    left_done(0)
    z_first(0)
    z_middle(0)
    z_prepare(0)
    left_spread(1)
    z_add(0)
    z_own(0)
    left_done(1)

    blocks = [(i, j) for i in range(4) for j in range(i, 4)]

    ltrue[...] = (
        dotb(left2[0], onehot[0], ((1,), (0,))) + dotb(left2[1], onehot[1], ((1,), (0,)))
    ).astype(BF)

    def left_block(i):
        return ltrue[:, B * i : B * i + B]

    for b, (i, j) in enumerate(blocks):
        gs[b] = dotb(left_block(i), left_block(j), ((0,), (0,)))

    def tile(j):
        return pl.ds(lax.rem(j, 2) * 5, 5), rows_at(c * 64 + lax.div(j, 2) * 8, 8, 8)

    gram_in = []
    for e, (dx, dz) in enumerate(plane):
        to = tile(mod4(x + dx) * 4 + mod4(z + dz))
        gram_in.append(send(gs.at[to], gr.at[e], peer(dx, dz), gr.at[e]))
    z_sum1(0)
    z_first(1)
    for wait in gram_in:
        wait()
    mine = tile(x * 4 + z)
    gram[mine] = gs[mine] + tree([gr[e] for e in range(15)] + [jnp.zeros((5, 8, B), F32)])
    gathered = []
    for dx, dz in plane:
        ref = gram.at[mine]
        gathered.append(send(ref, ref, peer(dx, dz), gram.at[tile(source_chip(dx, dz))]))
    z_middle(1)
    z_sum2(0)
    z_prepare(1)
    z_add(1)
    z_own(1)
    for wait in gathered:
        wait()
    ref = gram.at[:, rows_at(c * 64, 64)]
    pair_gram = send(ref, ref, sib, gram.at[:, rows_at((1 - c) * 64, 64)])
    z_forward(0, 0)
    pair_gram()

    on = lax.broadcasted_iota(jnp.int32, (B, B), 0) == lax.broadcasted_iota(jnp.int32, (B, B), 1)
    across, down = [], []
    for i in range(4):
        diag = jnp.where(on, gram[blocks.index((i, i))], 0.0)
        across.append(lax.rsqrt(jnp.sum(diag, axis=0, keepdims=True)))
        down.append(lax.rsqrt(jnp.sum(diag, axis=1, keepdims=True)))
    for i in range(4):
        for j in range(4):
            if j < i:
                block = jnp.zeros((B, B), F32)
            else:
                block = gram[blocks.index((i, j))] * down[i] * across[j]
            tmat[B * i : B * i + B, B * j : B * j + B] = block

    steps = {
        (0, 0): lambda: z_sum1(1),
        (0, 1): lambda: z_gather2(1, 0),
        (0, 2): lambda: z_gather2(3, 0),
        (0, 3): lambda: z_gather2(2, 0),
        (0, 7): lambda: z_last(0, 0),
        (1, 2): lambda: z_sum2(1),
        (1, 4): lambda: z_forward(3, 0),
        (1, 5): lambda: z_forward(1, 0),
        (1, 6): lambda: z_forward(2, 0),
        (2, 1): lambda: z_forward(0, 1),
        (2, 4): lambda: z_gather2(1, 1),
        (2, 5): lambda: z_gather2(3, 1),
        (2, 6): lambda: z_gather2(2, 1),
        (2, 7): lambda: z_last(3, 0),
        (3, 0): lambda: z_last(1, 0),
        (3, 1): lambda: z_last(2, 0),
        (3, 2): lambda: z_last(0, 1),
        (3, 7): lambda: z_forward(3, 1),
    }

    def hook(k, part):
        for (at, which), step in steps.items():
            if which == part:
                pl.when(k == at)(step)

    chol_inv(tmat, wmat, hook)
    ri = lax.broadcasted_iota(jnp.int32, (RANK, RANK), 0)
    ci = lax.broadcasted_iota(jnp.int32, (RANK, RANK), 1)
    tmat[...] = jnp.where(ci <= ri, tmat[...], 0.0) * jnp.concatenate(across, axis=1)
    w_hi, w_lo = [
        jnp.concatenate(
            [dotb(w, onehot[n], ((1,), (1,))).astype(BF) for n in range(2)], axis=1
        )
        for w in split(tmat[...])
    ]

    shard = zt_ref[sub_rows(p1, p2), :]
    right = dotb(shard, w_hi, ((1,), (1,))) + dotb(shard, w_lo, ((1,), (1,)))
    squares = jnp.sum(right * right, axis=0, keepdims=True)
    rows = [squares[:, B * i : B * i + B] for i in range(4)] + [jnp.zeros((4, B), F32)]
    nr1[0] = jnp.concatenate(rows, axis=0)
    norm_in = [
        send(nr1.at[0], nr1.at[e + 1], peer(dx, dz), nr1.at[e + 1])
        for e, (dx, dz) in enumerate(plane)
    ]
    z_forward(1, 1)
    own_left = jnp.concatenate([left2[0, my_rows, :], left2[1, my_rows, :]], axis=1)
    ortho = (dotb(own_left, w_hi, ((1,), (1,))) + dotb(own_left, w_lo, ((1,), (1,)))).astype(BF)
    z_forward(2, 1)
    feed[...] = (dotb(ortho, w_hi, ((1,), (0,))) + dotb(ortho, w_lo, ((1,), (0,)))).astype(BF)
    for wait in norm_in:
        wait()
    nr2[0] = tree([nr1[e] for e in range(16)])
    norm_in = [
        send(nr2.at[0], nr2.at[f + 1], member(dy, dc), nr2.at[f + 1])
        for f, (dy, dc) in enumerate(group)
    ]
    for d in (3, 1, 2):
        z_last(d, 1)
    for _, wait in zs.values():
        wait()

    for wait in swap_sent:
        wait()
    for n in range(COLS // 512):
        at = pl.ds(512 * n, 512)
        prod = dotb(feed[...], zt_ref[at, :], ((1,), (1,)))
        buf_ref[:, at] = (buf_ref[:, at].astype(F32) - 0.2 * prod).astype(BF)
    for wait in norm_in:
        wait()
    total = tree([nr2[f] for f in range(8)])
    total = jnp.concatenate([total[i : i + 1] for i in range(4)], axis=1)
    scale = lax.rsqrt(total + 1e-06)
    sub16 = lax.broadcasted_iota(jnp.int32, (16, RANK), 0)
    lane16 = lax.broadcasted_iota(jnp.int32, (16, RANK), 1)
    pick = jnp.where(lane16 == sub16 + r * 16, scale, 0.0)
    o_hi, o_lo = split(jnp.concatenate([ortho.astype(F32) * scale, pick], axis=0))
    lhs_ref[...] = (
        dotb(o_hi, w_hi, ((1,), (0,)))
        + (dotb(o_hi, w_lo, ((1,), (0,))) + dotb(o_lo, w_hi, ((1,), (0,))))
    ).astype(BF)
    for wait in sent:
        wait()


def gather_call(momentum, gradient, basis):
    anyspace = pl.BlockSpec(memory_space=pl.ANY)
    vmem = pl.BlockSpec(memory_space=pltpu.VMEM)
    scratch = [
        ((2, LOCAL, PART), BF),
        ((2, LOCAL, PART), BF),
        ((LOCAL, HALF), BF),
        ((HALF, 2 * LOCAL), BF),
        ((2, 256, HALF), BF),
        ((2, LOCAL, 256), F32),
        ((2, LOCAL, 256), BF),
        ((2, LOCAL, 256), BF),
        ((2, LOCAL, 256), BF),
        ((2, 3, 96, 256), BF),
        ((2, 2 * LOCAL, 256), BF),
        ((10, B, B), F32),
        ((15, 5, 8, B), F32),
        ((10, B, B), F32),
        ((RANK, RANK), F32),
        ((B, B), F32),
        ((2, 4, 2, SEG // 2, 256), BF),
        ((2, 2, SEG // 2, 256), F32),
        ((2, 2, SEG // 2, 256), F32),
        ((2, 2, SEG // 2, 256), BF),
        ((2, 2, 2, SEG // 2, 256), BF),
        ((2, 3, SUB, 256), BF),
        ((16, 8, B), F32),
        ((8, 8, B), F32),
        ((2, 256, RANK), BF),
        ((2 * LOCAL, RANK), BF),
        ((LOCAL, RANK), BF),
    ]
    return pl.pallas_call(
        gather_kernel,
        out_shape=(
            pltpu.VMEM((LOCAL, COLS), BF),
            pltpu.VMEM((COLS, RANK), BF),
            pltpu.VMEM((LOCAL + 16, RANK), BF),
        ),
        in_specs=[anyspace] * 3,
        out_specs=(vmem,) * 3,
        scratch_shapes=[pltpu.VMEM(s, t) for s, t in scratch]
        + [
            pltpu.SemaphoreType.DMA((9,)),
            pltpu.SemaphoreType.DMA((N_SEMS,)),
            pltpu.SemaphoreType.DMA((N_SEMS,)),
        ],
        compiler_params=pltpu.CompilerParams(
            collective_id=0, has_side_effects=True, vmem_limit_bytes=44 << 20
        ),
        name="project",
    )(momentum, gradient, basis)


def apply_kernel(mom_ref, zt_ref, lhs_ref, mom_hbm, bas_hbm, upd_hbm, bas, upd, sem):
    first = pltpu.make_async_copy(mom_ref, mom_hbm, sem.at[0])
    first.start()
    factor = math.sqrt(ROWS * WIDTH / RANK)
    copies = []
    for n in range(COLS // 512):
        at = pl.ds(512 * n, 512)
        prod = dotb(lhs_ref[...], zt_ref[at, :], ((1,), (1,)))
        upd[:, at] = (factor * prod[:LOCAL]).astype(BF)
        bas[:, at] = prod[LOCAL:].astype(BF)
        copies.append(pltpu.make_async_copy(upd.at[:, at], upd_hbm.at[:, at], sem.at[n + 2]))
        copies[-1].start()
    copies.append(pltpu.make_async_copy(bas, bas_hbm, sem.at[1]))
    copies[-1].start()
    first.wait()
    for copy in copies:
        copy.wait()


def apply_call(mom, zt, lhs):
    held = [pltpu.with_memory_space_constraint(v, pltpu.VMEM) for v in (mom, zt, lhs)]
    return pl.pallas_call(
        apply_kernel,
        out_shape=(
            jax.ShapeDtypeStruct((LOCAL, COLS), BF),
            jax.ShapeDtypeStruct((16, COLS), BF),
            jax.ShapeDtypeStruct((LOCAL, COLS), BF),
        ),
        in_specs=[pl.BlockSpec(memory_space=pltpu.VMEM)] * 3,
        out_specs=[pl.BlockSpec(memory_space=pl.ANY)] * 3,
        scratch_shapes=[
            pltpu.VMEM((16, COLS), BF),
            pltpu.VMEM((LOCAL, COLS), BF),
            pltpu.SemaphoreType.DMA((2 + COLS // 512,)),
        ],
        compiler_params=pltpu.CompilerParams(vmem_limit_bytes=24 << 20),
        name="apply",
    )(*held)


def local(momentum, gradient, basis):
    return apply_call(*gather_call(momentum, gradient, basis))


def solution(mesh):
    return jax.shard_map(
        local,
        mesh=mesh,
        in_specs=(P("rows", "cols"), P("rows", "cols"), P("rows", "cols")),
        out_specs=(P("rows", "cols"), P("rows", "cols"), P("rows", "cols")),
        check_vma=False,
    )
```

```python
import functools
import math

import jax
import jax.numpy as jnp
from jax import lax
from jax.experimental import pallas as pl
from jax.experimental.pallas import tpu as pltpu
from jax.sharding import PartitionSpec as P

ROWS = 12288
WIDTH = 26624
RANK = 512
MESH = pl.DeviceIdType.MESH
BF = jnp.bfloat16
F32 = jnp.float32

LOCAL = 384
COLS = 6656
HALF = 3328
PART = 1664
SEG = 832
SUB = 208
B = 128
N_SEMS = 224


def mod4(v):
    return lax.rem(v + 4, 4)


def rows_at(start, size, unit=16):
    return pl.ds(pl.multiple_of(start, unit), size)


def dotp(a, b, dims):
    return lax.dot_general(
        a, b, (dims, ((), ())), precision=lax.Precision.HIGHEST, preferred_element_type=F32
    )


def dotb(a, b, dims):
    return lax.dot_general(a, b, (dims, ((), ())), preferred_element_type=F32)


def split(a):
    hi = a.astype(BF)
    return hi, (a - hi.astype(F32)).astype(BF)


def tree(terms):
    while len(terms) > 1:
        terms = [a + b for a, b in zip(terms[::2], terms[1::2])]
    return terms[0]


def sweep(w_ref, t, hook):
    sub = lax.broadcasted_iota(jnp.int32, (8, B), 0)
    lane = lax.broadcasted_iota(jnp.int32, (8, B), 1)
    panels = B // 8
    for p in range(panels):
        top = t[:8]
        cols = jnp.stack(
            [jnp.broadcast_to(top[:, 8 * p + j : 8 * p + j + 1], (8, B)) for j in range(8)]
        )
        for j in range(0, 8, 2):
            d0 = jnp.broadcast_to(cols[j, j : j + 1, :], (8, B))
            off = jnp.broadcast_to(cols[j, j + 1 : j + 2, :], (8, B))
            d1 = jnp.broadcast_to(cols[j + 1, j + 1 : j + 2, :], (8, B))
            r0 = lax.rsqrt(d0)
            r1 = lax.rsqrt(d0 * d1 - off * off) * (d0 * r0)
            low = off * r0
            below = sub > j + 1
            m0 = jnp.where(below, cols[j] * r0, 0.0)
            m1 = jnp.where(below, (cols[j + 1] - m0 * low) * r1, 0.0)
            c0 = jnp.where(sub >= j, jnp.where(sub == j, 1.0, 0.0), cols[j])
            c1 = jnp.where(sub >= j, jnp.where(sub == j + 1, 1.0, 0.0), cols[j + 1])
            parts = [cols[:j]] if j else []
            parts += [c0[None], c1[None]]
            if j < 6:
                parts.append(cols[j + 2 :])
            cols = jnp.concatenate(parts, axis=0)
            s0 = cols[:, j : j + 1, :] * r0[None]
            s1 = (cols[:, j + 1 : j + 2, :] - low[None] * s0) * r1[None]
            rest = cols - m0[None] * s0 - m1[None] * s1
            cols = jnp.where((sub == j)[None], s0, jnp.where((sub == j + 1)[None], s1, rest))
        tri = [jnp.where(sub >= k, cols[k], 0.0) for k in range(8)]
        inside = (lane >= 8 * p) & (lane < 8 * p + 8)
        eye = jnp.where(inside, jnp.where(lane - 8 * p == sub, 1.0, 0.0), top)
        new = tree([tri[k] * eye[k : k + 1] for k in range(8)])
        w_ref[8 * p : 8 * p + 8, :] = jnp.where(lane <= sub + 8 * p, new, 0.0)
        if p < panels - 1:
            rest = t[8:]
            lanes = lax.broadcasted_iota(jnp.int32, rest.shape, 1)
            t = jnp.where((lanes >= 8 * p) & (lanes < 8 * p + 8), 0.0, rest)
            ys = [jnp.sum(tri[k] * new, axis=0, keepdims=True) for k in range(8)]
            t = t - tree([rest[:, 8 * p + k : 8 * p + k + 1] * ys[k] for k in range(8)])
        if p % 2 == 1:
            hook(p // 2)


def chol_inv(t_ref, w_ref, hook):
    lanes = lax.broadcasted_iota(jnp.int32, (B, RANK), 1)
    subs = lax.broadcasted_iota(jnp.int32, (B, RANK), 0)

    def block(k, carry):
        base = pl.multiple_of(k * B, B)
        rows = pl.ds(base, B)
        sweep(w_ref, t_ref[rows, rows], functools.partial(hook, k))
        own = (lanes >= base) & (lanes < base + B)
        mine = jnp.where(own, jnp.where(lanes - base == subs, 1.0, 0.0), t_ref[rows, :])
        new = dotp(w_ref[...], mine, ((1,), (0,)))
        t_ref[rows, :] = new

        def below(i, c):
            at = pl.ds(pl.multiple_of(i * B, B), B)
            t_ref[at, :] = jnp.where(own, 0.0, t_ref[at, :]) - dotp(
                t_ref[rows, at], new, ((0,), (0,))
            )
            return c

        lax.fori_loop(k + 1, RANK // B, below, 0)
        return carry

    lax.fori_loop(0, RANK // B, block, 0)


def gather_kernel(
    m_hbm, g_hbm, basis_hbm, buf_ref, zt_ref, lhs_ref,
    mbuf, gbuf, side, buf2t, bas, pleft, psend, precv, chip_left, yr, left2,
    gs, gr, gram, tmat, wmat, zp, zown, zl, zrh, zrf, zr2, nr1, nr2, onehot, ltrue,
    load_sem, send_sem, recv_sem,
):
    r = lax.axis_index("rows")
    y = lax.axis_index("cols")
    c = lax.rem(r, 2)
    z = lax.rem(lax.div(r, 2), 4)
    x = lax.div(r, 8)
    p1 = x * (1 - c) + z * c
    p2 = z * (1 - c) + x * c

    def chip(a, b):
        return a * (4 - 3 * c) + b * (1 + 3 * c)

    def device(a, b):
        return 2 * chip(a, b) + c

    sib = (r + 1 - 2 * c, y)
    a1p = (device(mod4(p1 + 1), p2), y)
    a1m = (device(mod4(p1 - 1), p2), y)
    a2p = (device(p1, mod4(p2 + 1)), y)
    a2m = (device(p1, mod4(p2 - 1)), y)
    plane = [(dx, dz) for dx in range(4) for dz in range(4) if dx or dz]

    def peer(dx, dz):
        return (mod4(x + dx) * 8 + mod4(z + dz) * 2 + c, y)

    def source_chip(dx, dz):
        return mod4(x - dx) * 4 + mod4(z - dz)

    group = [(dy, dc) for dy in range(4) for dc in range(2) if dy or dc]

    def member(dy, dc):
        return (r + dc * (1 - 2 * c), mod4(y + dy))

    count = [0]
    sent = []

    def plan(src, dst, to, landing):
        i = count[0]
        count[0] += 1

        def copy(s, d):
            return pltpu.make_async_remote_copy(
                s, d, send_sem.at[i], recv_sem.at[i], device_id=to, device_id_type=MESH
            )

        def start():
            copy(src, dst).start()
            sent.append(lambda: copy(src, dst).wait_send())

        return start, lambda: copy(landing, landing).wait_recv()

    def send(src, dst, to, landing):
        start, wait = plan(src, dst, to, landing)
        start()
        return wait

    def columns(core, part):
        return pl.ds(pl.multiple_of(core * HALF + part * PART, 128), PART)

    order = [(1 - c, 0), (1 - c, 1), (c, 0), (c, 1)]

    def load(n):
        at = columns(*order[n])
        return [
            pltpu.make_async_copy(m_hbm.at[:, at], mbuf.at[n % 2], load_sem.at[2 * n]),
            pltpu.make_async_copy(g_hbm.at[:, at], gbuf.at[n % 2], load_sem.at[2 * n + 1]),
        ]

    loads = [load(n) for n in range(4)]
    for n in range(2):
        for copy in loads[n]:
            copy.start()
    parts = [pl.ds(0, PART), pl.ds(PART, PART)]

    def half_of(core):
        return pl.ds(pl.multiple_of(core * HALF, 128), HALF)

    def chip_rows(a, b):
        return rows_at(chip(a, b) * 16, 16)

    here = chip_rows(p1, p2)
    own_basis = pltpu.make_async_copy(
        basis_hbm.at[:, half_of(c)], bas.at[c, here], load_sem.at[8]
    )
    own_basis.start()

    barrier = pltpu.get_barrier_semaphore()
    a1o = (device(mod4(p1 + 2), p2), y)
    others = [sib, a1p, a1m, a1o, a2p, a2m] + [(r, mod4(y + d)) for d in (1, 2, 3)]
    for to in others:
        pl.semaphore_signal(barrier, inc=1, device_id=to, device_id_type=MESH)
    pl.semaphore_wait(barrier, len(others))

    got = send(basis_hbm.at[:, half_of(1 - c)], bas.at[c, here], sib, bas.at[1 - c, here])

    def piece(a, b, n):
        return bas.at[n, chip_rows(a, b)]

    def half_piece(a, b, n, h):
        return bas.at[n, chip_rows(a, b), parts[h]]

    def at1(d):
        return mod4(p1 + d)

    def at2(d):
        return mod4(p2 + d)

    own_basis.wait()
    got()
    first = [None, None]
    second = [[], []]

    def both2(d, n):
        a = at1(d)
        ref = piece(a, p2, n)
        second[n].append(
            (
                send(ref, ref, a2p, piece(a, at2(-1), n)),
                send(ref, ref, a2m, piece(a, at2(1), n)),
            )
        )

    def start(n):
        mine = piece(p1, p2, n)
        first[n] = {
            d: send(mine, mine, to, piece(at1(d), p2, n))
            for d, to in ((-1, a1p), (1, a1m), (2, a1o))
        }
        both2(0, n)

    def pass_on(n):
        for d in (-1, 1, 2):
            first[n][d]()
            both2(d, n)

    start(0)
    start(1)

    def add_loaded(n):
        for copy in loads[n]:
            copy.wait()

        def step(i, carry):
            at = rows_at(i * 16, 16)
            total = mbuf[n % 2, at, :].astype(F32) + gbuf[n % 2, at, :].astype(F32)
            buf_ref[at, columns(*order[n])] = total.astype(BF)
            return carry

        lax.fori_loop(0, LOCAL // 16, step, 0)
        if n < 2:
            for copy in loads[n + 2]:
                copy.start()

    my_rows = rows_at(c * LOCAL, LOCAL, 128)
    sib_rows = rows_at((1 - c) * LOCAL, LOCAL, 128)

    def send_buffer(n):
        return send(
            buf_ref.at[:, columns(1 - c, n)], side.at[:, parts[n]], sib, side.at[:, parts[n]]
        )

    def turn(n, mine):
        def step(i, carry):
            at = rows_at(n * PART + i * 128, 128, 128)
            if mine:
                from_at = rows_at(c * HALF + n * PART + i * 128, 128, 128)
                buf2t[at, my_rows] = buf_ref[:, from_at].T
            else:
                buf2t[at, sib_rows] = side[:, at].T
            return carry

        lax.fori_loop(0, PART // 128, step, 0)

    last = [[], []]
    offsets = (0, -1, 1, 2)

    def forward2(n, q):
        a = at1(offsets[q])
        from_m, from_p = second[n][q]
        from_m()
        ref = half_piece(a, at2(-1), n, 0)
        last[n].append(send(ref, ref, a2p, half_piece(a, at2(2), n, 0)))
        from_p()
        ref = half_piece(a, at2(1), n, 1)
        last[n].append(send(ref, ref, a2m, half_piece(a, at2(2), n, 1)))

    ranks = [pl.ds(0, 256), pl.ds(256, 256)]

    def sub_rows(a, b):
        return rows_at(c * HALF + a * SEG + b * SUB, SUB)

    def sub_half(a, b, h):
        return rows_at(c * HALF + a * SEG + b * SUB + 112 * h, 112 - 16 * h)

    def to_sib(a, d, s):
        ref = zt_ref.at[sub_rows(at1(a), at2(d)), ranks[s]]
        start = (1 - c) * HALF + at2(a) * SEG + at1(d) * SUB
        return plan(ref, ref, sib, zt_ref.at[rows_at(start, SUB), ranks[s]])

    def part(b, s):
        return zp.at[s, 0, lax.div(b, 2), rows_at(lax.rem(b, 2) * SUB, SUB)]

    z2, z3, z4, z5, zs = {}, {}, {}, {}, {}
    for s in range(2):

        def sub(a, b, s=s):
            return zt_ref.at[sub_rows(a, b), ranks[s]]

        def half(a, b, h, s=s):
            return zt_ref.at[sub_half(a, b, h), ranks[s]]

        own = sub(p1, p2)
        for d in (2, 1, 3):
            to = (device(p1, at2(d)), y)
            z2[s, d] = plan(part(at2(d), s), zr2.at[s, d - 1], to, zr2.at[s, d - 1])
            z3[s, d] = plan(own, own, to, sub(p1, at2(-d)))
        for d in range(4):
            b = at2(d)
            ref = sub(p1, b)
            z4[s, d] = (
                plan(ref, ref, a1p, sub(at1(-1), b)),
                plan(ref, ref, a1m, sub(at1(1), b)),
            )
            ref, ref1 = half(at1(-1), b, 0), half(at1(1), b, 1)
            z5[s, d] = (
                plan(ref, ref, a1p, half(at1(2), b, 0)),
                plan(ref1, ref1, a1m, half(at1(2), b, 1)),
            )
            for a in range(4):
                zs[s, a, d] = to_sib(a, d, s)

    def z_sum1(s):
        for wait in z_full[s]:
            wait()

        def step(i, carry):
            h, at = lax.div(i, 2), rows_at(lax.rem(i, 2) * SUB, SUB)
            total = zown[s, h, at, :] + zrf[s, 0, h, at, :].astype(F32)
            total = total + zrf[s, 1, h, at, :].astype(F32)
            zp[s, 0, h, at, :] = total.astype(BF)
            return carry

        lax.fori_loop(0, 4, step, 0)
        for d in (2, 1, 3):
            z2[s, d][0]()

    def z_out(d, s):
        z4[s, d][0][0]()
        z4[s, d][1][0]()
        zs[s, 0, d][0]()

    def z_sum2(s):
        for d in (1, 3, 2):
            z2[s, d][1]()
        total = zp[s, 0, lax.div(p2, 2), rows_at(lax.rem(p2, 2) * SUB, SUB), :].astype(F32)
        for d in range(3):
            total = total + zr2[s, d].astype(F32)
        zt_ref[sub_rows(p1, p2), ranks[s]] = total.astype(BF)
        for d in (2, 1, 3):
            z3[s, d][0]()
        z_out(0, s)

    def z_gather2(d, s):
        z3[s, d][1]()
        z_out((4 - d) % 4, s)

    def z_forward(d, s):
        (_, from_m), (_, from_p) = z4[s, d]
        from_m()
        z5[s, d][0][0]()
        zs[s, 3, d][0]()
        from_p()
        z5[s, d][1][0]()
        zs[s, 1, d][0]()

    def z_last(d, s):
        for _, wait in z5[s, d]:
            wait()
        zs[s, 2, d][0]()

    for n in range(2):
        k = lax.broadcasted_iota(jnp.int32, (256, RANK), 0)
        rank = lax.shift_right_logical(k, 4) * 32 + (k & 15) + 16 * n
        hit = lax.broadcasted_iota(jnp.int32, (256, RANK), 1) == rank
        onehot[n] = jnp.where(hit, 1.0, 0.0).astype(BF)

    paired, summed, spread, pairs = [], [], [], []

    def left_pair(s):
        for wait in last[s]:
            wait()
        psend[s] = dotb(side[...], bas[s], ((1,), (1,))).astype(BF)
        paired.append(send(psend.at[s], precv.at[s], sib, precv.at[s]))
        pleft[s] = dotb(buf_ref[:, half_of(c)], bas[s], ((1,), (1,)))

    def along_y(d):
        return (r, mod4(y + d))

    def left_rows(core, d):
        return rows_at(core * LOCAL + mod4(y + d) * 96, 96)

    def left_sum(s):
        paired[s]()
        total = pleft[s] + precv[s].astype(F32)
        pleft[s] = total
        chip_left[s] = total.astype(BF)
        summed.append(
            [
                send(
                    chip_left.at[s, rows_at(mod4(y + d) * 96, 96)],
                    yr.at[s, d - 1],
                    along_y(d),
                    yr.at[s, d - 1],
                )
                for d in (2, 1, 3)
            ]
        )

    def left_spread(s):
        for wait in summed[s]:
            wait()
        total = pleft[s, rows_at(y * 96, 96), :]
        for d in range(3):
            total = total + yr[s, d].astype(F32)
        left2[s, left_rows(c, 0), :] = total.astype(BF)
        ref = left2.at[s, left_rows(c, 0)]
        spread.append(
            {d: send(ref, ref, along_y(d), left2.at[s, left_rows(c, -d)]) for d in (2, 1, 3)}
        )
        pairs.append([send(ref, ref, sib, left2.at[s, left_rows(1 - c, 0)])])

    def left_done(s):
        for d in (1, 3, 2):
            spread[s][d]()
            ref = left2.at[s, left_rows(c, -d)]
            pairs[s].append(send(ref, ref, sib, left2.at[s, left_rows(1 - c, -d)]))
        for wait in pairs[s]:
            wait()

    def z_value(d, h, s):
        at = rows_at(mod4(p1 + d) * SEG + (SEG // 2) * h, SEG // 2)
        return dotb(buf2t[at, :], left2[s], ((1,), (0,)))

    ways = (a1p, a1m)
    z_half = [[], []]
    z_full = [[], []]

    def z_first(s):
        for w in range(2):
            zp[s, 2, w] = z_value(2, w, s).astype(BF)
            z_half[s].append(send(zp.at[s, 2, w], zrh.at[s, w], ways[w], zrh.at[s, w]))

    def z_middle(s):
        for w, (d, h) in enumerate(((1, 1), (3, 0))):
            zp[s, d, h] = z_value(d, h, s).astype(BF)
            z_full[s].append(send(zp.at[s, d, h], zrf.at[s, w, h], ways[w], zrf.at[s, w, h]))

    def z_prepare(s):
        for w, (d, h) in enumerate(((1, 0), (3, 1))):
            zl[s, w] = z_value(d, h, s)

    def z_add(s):
        for w, (d, h) in enumerate(((1, 0), (3, 1))):
            z_half[s][w]()
            zp[s, d, h] = (zl[s, w] + zrh[s, w].astype(F32)).astype(BF)
            z_full[s].append(send(zp.at[s, d, h], zrf.at[s, w, h], ways[w], zrf.at[s, w, h]))

    def z_own(s):
        for h in range(2):
            zown[s, h] = z_value(0, h, s)

    add_loaded(0)
    swapped = [send_buffer(0)]
    add_loaded(1)
    swapped.append(send_buffer(1))
    add_loaded(2)
    add_loaded(3)
    pass_on(0)
    turn(0, True)
    pass_on(1)
    turn(1, True)
    forward2(0, 0)
    forward2(1, 0)
    for wait in swapped:
        wait()
    turn(0, False)
    forward2(0, 1)
    turn(1, False)
    forward2(0, 2)
    forward2(0, 3)
    forward2(1, 1)
    forward2(1, 2)
    forward2(1, 3)
    left_pair(0)
    left_sum(0)
    left_pair(1)
    left_sum(1)
    left_spread(0)
    left_spread(1)
    left_done(0)
    z_first(0)
    z_middle(0)
    left_done(1)

    blocks = [(i, j) for i in range(4) for j in range(i, 4)]

    ltrue[...] = (
        dotb(left2[0], onehot[0], ((1,), (0,))) + dotb(left2[1], onehot[1], ((1,), (0,)))
    ).astype(BF)

    def left_block(i):
        return ltrue[:, B * i : B * i + B]

    for b, (i, j) in enumerate(blocks):
        gs[b] = dotb(left_block(i), left_block(j), ((0,), (0,))).astype(BF)
    for b in (10, 11):
        gs[b] = jnp.zeros((B, B), BF)

    def tile(j):
        return pl.ds(lax.rem(j, 4) * 3, 3), rows_at(c * 64 + lax.div(j, 4) * 16, 16)

    gram_in = []
    for e, (dx, dz) in enumerate(plane):
        to = tile(mod4(x + dx) * 4 + mod4(z + dz))
        gram_in.append(send(gs.at[to], gr.at[e], peer(dx, dz), gr.at[e]))
    z_prepare(0)
    z_add(0)
    z_first(1)
    z_middle(1)
    for wait in gram_in:
        wait()
    mine = tile(x * 4 + z)
    gram[mine] = tree([v.astype(F32) for v in [gs[mine]] + [gr[e] for e in range(15)]]).astype(BF)
    gathered = []
    for dx, dz in plane:
        ref = gram.at[mine]
        gathered.append(send(ref, ref, peer(dx, dz), gram.at[tile(source_chip(dx, dz))]))
    z_prepare(1)
    z_own(0)
    z_own(1)
    z_sum1(0)
    z_add(1)
    for wait in gathered:
        wait()
    ref = gram.at[:, rows_at(c * 64, 64)]
    pair_gram = send(ref, ref, sib, gram.at[:, rows_at((1 - c) * 64, 64)])
    pair_gram()

    on = lax.broadcasted_iota(jnp.int32, (B, B), 0) == lax.broadcasted_iota(jnp.int32, (B, B), 1)
    across, down = [], []
    for i in range(4):
        diag = jnp.where(on, gram[blocks.index((i, i))].astype(F32), 0.0)
        across.append(lax.rsqrt(jnp.sum(diag, axis=0, keepdims=True)))
        down.append(lax.rsqrt(jnp.sum(diag, axis=1, keepdims=True)))
    for i in range(4):
        for j in range(4):
            if j < i:
                block = jnp.zeros((B, B), F32)
            else:
                block = gram[blocks.index((i, j))].astype(F32) * down[i] * across[j]
            tmat[B * i : B * i + B, B * j : B * j + B] = block

    steps = {
        (0, 0): lambda: z_sum2(0),
        (0, 5): lambda: z_sum1(1),
        (1, 1): lambda: z_forward(0, 0),
        (1, 4): lambda: z_gather2(1, 0),
        (1, 5): lambda: z_gather2(3, 0),
        (1, 6): lambda: z_gather2(2, 0),
        (2, 0): lambda: z_sum2(1),
        (2, 1): lambda: z_last(0, 0),
        (2, 7): lambda: z_forward(3, 0),
        (3, 0): lambda: z_forward(1, 0),
        (3, 1): lambda: z_forward(2, 0),
        (3, 2): lambda: z_forward(0, 1),
        (3, 3): lambda: z_gather2(1, 1),
        (3, 4): lambda: z_gather2(3, 1),
        (3, 5): lambda: z_gather2(2, 1),
        (3, 7): lambda: z_last(3, 0),
    }

    def hook(k, part):
        for (at, which), step in steps.items():
            if which == part:
                pl.when(k == at)(step)

    chol_inv(tmat, wmat, hook)
    ri = lax.broadcasted_iota(jnp.int32, (RANK, RANK), 0)
    ci = lax.broadcasted_iota(jnp.int32, (RANK, RANK), 1)
    tmat[...] = jnp.where(ci <= ri, tmat[...], 0.0) * jnp.concatenate(across, axis=1)
    w_hi, w_lo = [
        jnp.concatenate(
            [dotb(w, onehot[n], ((1,), (1,))).astype(BF) for n in range(2)], axis=1
        )
        for w in split(tmat[...])
    ]

    shard = zt_ref[sub_rows(p1, p2), :]
    right = dotb(shard, w_hi, ((1,), (1,))) + dotb(shard, w_lo, ((1,), (1,)))
    squares = jnp.sum(right * right, axis=0, keepdims=True)
    rows = [squares[:, B * i : B * i + B] for i in range(4)] + [jnp.zeros((4, B), F32)]
    nr1[0] = jnp.concatenate(rows, axis=0)
    norm_in = [
        send(nr1.at[0], nr1.at[e + 1], peer(dx, dz), nr1.at[e + 1])
        for e, (dx, dz) in enumerate(plane)
    ]
    z_last(1, 0)
    z_last(2, 0)
    z_last(0, 1)
    z_forward(3, 1)
    z_forward(1, 1)
    own_left = jnp.concatenate([left2[0, my_rows, :], left2[1, my_rows, :]], axis=1)
    ortho = (dotb(own_left, w_hi, ((1,), (1,))) + dotb(own_left, w_lo, ((1,), (1,)))).astype(BF)
    z_forward(2, 1)
    lhs_ref[:LOCAL, :] = (
        dotb(ortho, w_hi, ((1,), (0,))) + dotb(ortho, w_lo, ((1,), (0,)))
    ).astype(BF)
    for wait in norm_in:
        wait()
    nr2[0] = tree([nr1[e] for e in range(16)])
    norm_in = [
        send(nr2.at[0], nr2.at[f + 1], member(dy, dc), nr2.at[f + 1])
        for f, (dy, dc) in enumerate(group)
    ]
    for d in (3, 1, 2):
        z_last(d, 1)
    for wait in norm_in:
        wait()
    total = tree([nr2[f] for f in range(8)])
    total = jnp.concatenate([total[i : i + 1] for i in range(4)], axis=1)
    scale = lax.rsqrt(total + 1e-06)
    sub16 = lax.broadcasted_iota(jnp.int32, (16, RANK), 0)
    lane16 = lax.broadcasted_iota(jnp.int32, (16, RANK), 1)
    pick = jnp.where(lane16 == sub16 + r * 16, scale, 0.0)
    o_hi, o_lo = split(jnp.concatenate([ortho.astype(F32) * scale, pick], axis=0))
    lhs_ref[LOCAL:, :] = (
        dotb(o_hi, w_hi, ((1,), (0,)))
        + (dotb(o_hi, w_lo, ((1,), (0,))) + dotb(o_lo, w_hi, ((1,), (0,))))
    ).astype(BF)
    for _, wait in zs.values():
        wait()
    for wait in sent:
        wait()


def gather_call(momentum, gradient, basis):
    anyspace = pl.BlockSpec(memory_space=pl.ANY)
    vmem = pl.BlockSpec(memory_space=pltpu.VMEM)
    scratch = [
        ((2, LOCAL, PART), BF),
        ((2, LOCAL, PART), BF),
        ((LOCAL, HALF), BF),
        ((HALF, 2 * LOCAL), BF),
        ((2, 256, HALF), BF),
        ((2, LOCAL, 256), F32),
        ((2, LOCAL, 256), BF),
        ((2, LOCAL, 256), BF),
        ((2, LOCAL, 256), BF),
        ((2, 3, 96, 256), BF),
        ((2, 2 * LOCAL, 256), BF),
        ((12, B, B), BF),
        ((15, 3, 16, B), BF),
        ((12, B, B), BF),
        ((RANK, RANK), F32),
        ((B, B), F32),
        ((2, 4, 2, SEG // 2, 256), BF),
        ((2, 2, SEG // 2, 256), F32),
        ((2, 2, SEG // 2, 256), F32),
        ((2, 2, SEG // 2, 256), BF),
        ((2, 2, 2, SEG // 2, 256), BF),
        ((2, 3, SUB, 256), BF),
        ((16, 8, B), F32),
        ((8, 8, B), F32),
        ((2, 256, RANK), BF),
        ((2 * LOCAL, RANK), BF),
    ]
    return pl.pallas_call(
        gather_kernel,
        out_shape=(
            pltpu.VMEM((LOCAL, COLS), BF),
            pltpu.VMEM((COLS, RANK), BF),
            pltpu.VMEM((2 * LOCAL + 16, RANK), BF),
        ),
        in_specs=[anyspace] * 3,
        out_specs=(vmem,) * 3,
        scratch_shapes=[pltpu.VMEM(s, t) for s, t in scratch]
        + [
            pltpu.SemaphoreType.DMA((9,)),
            pltpu.SemaphoreType.DMA((N_SEMS,)),
            pltpu.SemaphoreType.DMA((N_SEMS,)),
        ],
        compiler_params=pltpu.CompilerParams(
            collective_id=0, has_side_effects=True, vmem_limit_bytes=44 << 20
        ),
        name="project",
    )(momentum, gradient, basis)


def apply_kernel(buf_ref, zt_ref, lhs_ref, mom_hbm, bas_hbm, upd_hbm, mom, bas, upd, sem):
    factor = math.sqrt(ROWS * WIDTH / RANK)
    copies = []

    def write(n, src, dst):
        copies.append(pltpu.make_async_copy(src, dst, sem.at[n]))
        copies[-1].start()

    for n in range(COLS // 512):
        at = pl.ds(512 * n, 512)
        prod = dotb(lhs_ref[...], zt_ref[at, :], ((1,), (1,)))
        mom[:, at] = (buf_ref[:, at].astype(F32) - 0.2 * prod[:LOCAL]).astype(BF)
        write(2 * n, mom.at[:, at], mom_hbm.at[:, at])
        upd[:, at] = (factor * prod[LOCAL : 2 * LOCAL]).astype(BF)
        write(2 * n + 1, upd.at[:, at], upd_hbm.at[:, at])
        bas[:, at] = prod[2 * LOCAL :].astype(BF)
    write(2 * (COLS // 512), bas, bas_hbm)
    for copy in copies:
        copy.wait()


def apply_call(buf, zt, lhs):
    held = [pltpu.with_memory_space_constraint(v, pltpu.VMEM) for v in (buf, zt, lhs)]
    return pl.pallas_call(
        apply_kernel,
        out_shape=(
            jax.ShapeDtypeStruct((LOCAL, COLS), BF),
            jax.ShapeDtypeStruct((16, COLS), BF),
            jax.ShapeDtypeStruct((LOCAL, COLS), BF),
        ),
        in_specs=[pl.BlockSpec(memory_space=pltpu.VMEM)] * 3,
        out_specs=[pl.BlockSpec(memory_space=pl.ANY)] * 3,
        scratch_shapes=[
            pltpu.VMEM((LOCAL, COLS), BF),
            pltpu.VMEM((16, COLS), BF),
            pltpu.VMEM((LOCAL, COLS), BF),
            pltpu.SemaphoreType.DMA((1 + 2 * (COLS // 512),)),
        ],
        compiler_params=pltpu.CompilerParams(vmem_limit_bytes=30 << 20),
        name="apply",
    )(*held)


def local(momentum, gradient, basis):
    return apply_call(*gather_call(momentum, gradient, basis))


def solution(mesh):
    return jax.shard_map(
        local,
        mesh=mesh,
        in_specs=(P("rows", "cols"), P("rows", "cols"), P("rows", "cols")),
        out_specs=(P("rows", "cols"), P("rows", "cols"), P("rows", "cols")),
        check_vma=False,
    )
```

```python
import functools
import math

import jax
import jax.numpy as jnp
from jax import lax
from jax.experimental import pallas as pl
from jax.experimental.pallas import tpu as pltpu
from jax.sharding import PartitionSpec as P

ROWS = 12288
WIDTH = 26624
RANK = 512
MESH = pl.DeviceIdType.MESH
BF = jnp.bfloat16
F32 = jnp.float32

LOCAL = 384
COLS = 6656
HALF = 3328
PART = 1664
SEG = 832
SUB = 208
B = 128
N_SEMS = 224


def mod4(v):
    return lax.rem(v + 4, 4)


def rows_at(start, size, unit=16):
    return pl.ds(pl.multiple_of(start, unit), size)


def dotp(a, b, dims):
    return lax.dot_general(
        a, b, (dims, ((), ())), precision=lax.Precision.HIGHEST, preferred_element_type=F32
    )


def dotb(a, b, dims):
    return lax.dot_general(a, b, (dims, ((), ())), preferred_element_type=F32)


def split(a):
    hi = a.astype(BF)
    return hi, (a - hi.astype(F32)).astype(BF)


def tree(terms):
    while len(terms) > 1:
        terms = [a + b for a, b in zip(terms[::2], terms[1::2])]
    return terms[0]


def sweep(w_ref, t, hook):
    sub = lax.broadcasted_iota(jnp.int32, (8, B), 0)
    lane = lax.broadcasted_iota(jnp.int32, (8, B), 1)
    panels = B // 8
    for p in range(panels):
        top = t[:8]
        cols = jnp.stack(
            [jnp.broadcast_to(top[:, 8 * p + j : 8 * p + j + 1], (8, B)) for j in range(8)]
        )
        for j in range(0, 8, 2):
            d0 = jnp.broadcast_to(cols[j, j : j + 1, :], (8, B))
            off = jnp.broadcast_to(cols[j, j + 1 : j + 2, :], (8, B))
            d1 = jnp.broadcast_to(cols[j + 1, j + 1 : j + 2, :], (8, B))
            r0 = lax.rsqrt(d0)
            r1 = lax.rsqrt(d0 * d1 - off * off) * (d0 * r0)
            low = off * r0
            below = sub > j + 1
            m0 = jnp.where(below, cols[j] * r0, 0.0)
            m1 = jnp.where(below, (cols[j + 1] - m0 * low) * r1, 0.0)
            c0 = jnp.where(sub >= j, jnp.where(sub == j, 1.0, 0.0), cols[j])
            c1 = jnp.where(sub >= j, jnp.where(sub == j + 1, 1.0, 0.0), cols[j + 1])
            parts = [cols[:j]] if j else []
            parts += [c0[None], c1[None]]
            if j < 6:
                parts.append(cols[j + 2 :])
            cols = jnp.concatenate(parts, axis=0)
            s0 = cols[:, j : j + 1, :] * r0[None]
            s1 = (cols[:, j + 1 : j + 2, :] - low[None] * s0) * r1[None]
            rest = cols - m0[None] * s0 - m1[None] * s1
            cols = jnp.where((sub == j)[None], s0, jnp.where((sub == j + 1)[None], s1, rest))
        tri = [jnp.where(sub >= k, cols[k], 0.0) for k in range(8)]
        inside = (lane >= 8 * p) & (lane < 8 * p + 8)
        eye = jnp.where(inside, jnp.where(lane - 8 * p == sub, 1.0, 0.0), top)
        new = tree([tri[k] * eye[k : k + 1] for k in range(8)])
        w_ref[8 * p : 8 * p + 8, :] = jnp.where(lane <= sub + 8 * p, new, 0.0)
        if p < panels - 1:
            rest = t[8:]
            lanes = lax.broadcasted_iota(jnp.int32, rest.shape, 1)
            t = jnp.where((lanes >= 8 * p) & (lanes < 8 * p + 8), 0.0, rest)
            ys = [jnp.sum(tri[k] * new, axis=0, keepdims=True) for k in range(8)]
            t = t - tree([rest[:, 8 * p + k : 8 * p + k + 1] * ys[k] for k in range(8)])
        if p % 2 == 1:
            hook(p // 2)


def chol_inv(t_ref, w_ref, hook):
    lanes = lax.broadcasted_iota(jnp.int32, (B, RANK), 1)
    subs = lax.broadcasted_iota(jnp.int32, (B, RANK), 0)

    def block(k, carry):
        base = pl.multiple_of(k * B, B)
        rows = pl.ds(base, B)
        sweep(w_ref, t_ref[rows, rows], functools.partial(hook, k))
        own = (lanes >= base) & (lanes < base + B)
        mine = jnp.where(own, jnp.where(lanes - base == subs, 1.0, 0.0), t_ref[rows, :])
        new = dotp(w_ref[...], mine, ((1,), (0,)))
        t_ref[rows, :] = new

        def below(i, c):
            at = pl.ds(pl.multiple_of(i * B, B), B)
            t_ref[at, :] = jnp.where(own, 0.0, t_ref[at, :]) - dotp(
                t_ref[rows, at], new, ((0,), (0,))
            )
            return c

        lax.fori_loop(k + 1, RANK // B, below, 0)
        return carry

    lax.fori_loop(0, RANK // B, block, 0)


def gather_kernel(
    m_hbm, g_hbm, basis_hbm, buf_ref, zt_ref, lhs_ref,
    mbuf, gbuf, side, buf2t, bas, pleft, psend, precv, chip_left, yr, left2,
    gs, gr, gram, tmat, wmat, zp, zown, zl, zrh, zrf, zr2, nr1, nr2, onehot, ltrue,
    load_sem, send_sem, recv_sem,
):
    r = lax.axis_index("rows")
    y = lax.axis_index("cols")
    c = lax.rem(r, 2)
    z = lax.rem(lax.div(r, 2), 4)
    x = lax.div(r, 8)
    p1 = x * (1 - c) + z * c
    p2 = z * (1 - c) + x * c

    def chip(a, b):
        return a * (4 - 3 * c) + b * (1 + 3 * c)

    def device(a, b):
        return 2 * chip(a, b) + c

    sib = (r + 1 - 2 * c, y)
    a1p = (device(mod4(p1 + 1), p2), y)
    a1m = (device(mod4(p1 - 1), p2), y)
    a2p = (device(p1, mod4(p2 + 1)), y)
    a2m = (device(p1, mod4(p2 - 1)), y)
    plane = [(dx, dz) for dx in range(4) for dz in range(4) if dx or dz]

    def peer(dx, dz):
        return (mod4(x + dx) * 8 + mod4(z + dz) * 2 + c, y)

    def source_chip(dx, dz):
        return mod4(x - dx) * 4 + mod4(z - dz)

    group = [(dy, dc) for dy in range(4) for dc in range(2) if dy or dc]

    def member(dy, dc):
        return (r + dc * (1 - 2 * c), mod4(y + dy))

    count = [0]
    sent = []

    def plan(src, dst, to, landing):
        i = count[0]
        count[0] += 1

        def copy(s, d):
            return pltpu.make_async_remote_copy(
                s, d, send_sem.at[i], recv_sem.at[i], device_id=to, device_id_type=MESH
            )

        def start():
            copy(src, dst).start()
            sent.append(lambda: copy(src, dst).wait_send())

        return start, lambda: copy(landing, landing).wait_recv()

    def send(src, dst, to, landing):
        start, wait = plan(src, dst, to, landing)
        start()
        return wait

    def drain(n):
        for wait in sent[:n]:
            wait()
        del sent[:n]

    def columns(core, part):
        return pl.ds(pl.multiple_of(core * HALF + part * PART, 128), PART)

    order = [(1 - c, 0), (1 - c, 1), (c, 0), (c, 1)]

    def load(n):
        at = columns(*order[n])
        return [
            pltpu.make_async_copy(m_hbm.at[:, at], mbuf.at[n % 2], load_sem.at[2 * n]),
            pltpu.make_async_copy(g_hbm.at[:, at], gbuf.at[n % 2], load_sem.at[2 * n + 1]),
        ]

    loads = [load(n) for n in range(4)]
    for n in range(2):
        for copy in loads[n]:
            copy.start()
    parts = [pl.ds(0, PART), pl.ds(PART, PART)]

    def half_of(core):
        return pl.ds(pl.multiple_of(core * HALF, 128), HALF)

    def chip_rows(a, b):
        return rows_at(chip(a, b) * 16, 16)

    here = chip_rows(p1, p2)
    own_basis = pltpu.make_async_copy(
        basis_hbm.at[:, half_of(c)], bas.at[c, here], load_sem.at[8]
    )
    own_basis.start()

    barrier = pltpu.get_barrier_semaphore()
    a1o = (device(mod4(p1 + 2), p2), y)
    others = [sib, a1p, a1m, a1o, a2p, a2m] + [(r, mod4(y + d)) for d in (1, 2, 3)]
    for to in others:
        pl.semaphore_signal(barrier, inc=1, device_id=to, device_id_type=MESH)
    pl.semaphore_wait(barrier, len(others))

    got = send(basis_hbm.at[:, half_of(1 - c)], bas.at[c, here], sib, bas.at[1 - c, here])

    def piece(a, b, n):
        return bas.at[n, chip_rows(a, b)]

    def half_piece(a, b, n, h):
        return bas.at[n, chip_rows(a, b), parts[h]]

    def at1(d):
        return mod4(p1 + d)

    def at2(d):
        return mod4(p2 + d)

    own_basis.wait()
    got()
    first = [None, None]
    second = [[], []]

    def both2(d, n):
        a = at1(d)
        ref = piece(a, p2, n)
        second[n].append(
            (
                send(ref, ref, a2p, piece(a, at2(-1), n)),
                send(ref, ref, a2m, piece(a, at2(1), n)),
            )
        )

    def start(n):
        mine = piece(p1, p2, n)
        first[n] = {
            d: send(mine, mine, to, piece(at1(d), p2, n))
            for d, to in ((-1, a1p), (1, a1m), (2, a1o))
        }
        both2(0, n)

    def pass_on(n):
        for d in (-1, 1, 2):
            first[n][d]()
            both2(d, n)

    start(0)
    start(1)

    def add_loaded(n):
        for copy in loads[n]:
            copy.wait()

        def step(i, carry):
            at = rows_at(i * 16, 16)
            total = mbuf[n % 2, at, :].astype(F32) + gbuf[n % 2, at, :].astype(F32)
            buf_ref[at, columns(*order[n])] = total.astype(BF)
            return carry

        lax.fori_loop(0, LOCAL // 16, step, 0)
        if n < 2:
            for copy in loads[n + 2]:
                copy.start()

    my_rows = rows_at(c * LOCAL, LOCAL, 128)
    sib_rows = rows_at((1 - c) * LOCAL, LOCAL, 128)

    def send_buffer(n):
        return send(
            buf_ref.at[:, columns(1 - c, n)], side.at[:, parts[n]], sib, side.at[:, parts[n]]
        )

    def turn(n, mine):
        def step(i, carry):
            at = rows_at(n * PART + i * 128, 128, 128)
            if mine:
                from_at = rows_at(c * HALF + n * PART + i * 128, 128, 128)
                buf2t[at, my_rows] = buf_ref[:, from_at].T
            else:
                buf2t[at, sib_rows] = side[:, at].T
            return carry

        lax.fori_loop(0, PART // 128, step, 0)

    last = [[], []]
    offsets = (0, -1, 1, 2)

    def forward2(n, q):
        a = at1(offsets[q])
        from_m, from_p = second[n][q]
        from_m()
        ref = half_piece(a, at2(-1), n, 0)
        last[n].append(send(ref, ref, a2p, half_piece(a, at2(2), n, 0)))
        from_p()
        ref = half_piece(a, at2(1), n, 1)
        last[n].append(send(ref, ref, a2m, half_piece(a, at2(2), n, 1)))

    def sub_rows(a, b):
        return rows_at(c * HALF + a * SEG + b * SUB, SUB)

    def sub_half(a, b, h):
        return rows_at(c * HALF + a * SEG + b * SUB + 112 * h, 112 - 16 * h)

    def to_sib(a, d, s):
        ref = zt_ref.at[s, sub_rows(at1(a), at2(d))]
        start = (1 - c) * HALF + at2(a) * SEG + at1(d) * SUB
        return plan(ref, ref, sib, zt_ref.at[s, rows_at(start, SUB)])

    def part(b, s):
        return zp.at[s, 0, lax.div(b, 2), rows_at(lax.rem(b, 2) * SUB, SUB)]

    z2, z3, z4, z5, zs = {}, {}, {}, {}, {}
    for s in range(2):

        def sub(a, b, s=s):
            return zt_ref.at[s, sub_rows(a, b)]

        def half(a, b, h, s=s):
            return zt_ref.at[s, sub_half(a, b, h)]

        own = sub(p1, p2)
        for d in (2, 1, 3):
            to = (device(p1, at2(d)), y)
            z2[s, d] = plan(part(at2(d), s), zr2.at[s, d - 1], to, zr2.at[s, d - 1])
            z3[s, d] = plan(own, own, to, sub(p1, at2(-d)))
        for d in range(4):
            b = at2(d)
            ref = sub(p1, b)
            z4[s, d] = (
                plan(ref, ref, a1p, sub(at1(-1), b)),
                plan(ref, ref, a1m, sub(at1(1), b)),
            )
            ref, ref1 = half(at1(-1), b, 0), half(at1(1), b, 1)
            z5[s, d] = (
                plan(ref, ref, a1p, half(at1(2), b, 0)),
                plan(ref1, ref1, a1m, half(at1(2), b, 1)),
            )
            for a in range(4):
                zs[s, a, d] = to_sib(a, d, s)

    def z_sum1(s):
        for wait in z_full[s]:
            wait()

        def step(i, carry):
            h, at = lax.div(i, 2), rows_at(lax.rem(i, 2) * SUB, SUB)
            total = zown[s, h, at, :] + zrf[s, 0, h, at, :].astype(F32)
            total = total + zrf[s, 1, h, at, :].astype(F32)
            zp[s, 0, h, at, :] = total.astype(BF)
            return carry

        lax.fori_loop(0, 4, step, 0)
        for d in (2, 1, 3):
            z2[s, d][0]()

    def z_out(d, s):
        z4[s, d][0][0]()
        z4[s, d][1][0]()
        zs[s, 0, d][0]()

    def z_sum2(s):
        for d in (1, 3, 2):
            z2[s, d][1]()
        total = zp[s, 0, lax.div(p2, 2), rows_at(lax.rem(p2, 2) * SUB, SUB), :].astype(F32)
        for d in range(3):
            total = total + zr2[s, d].astype(F32)
        zt_ref[s, sub_rows(p1, p2), :] = total.astype(BF)
        for d in (2, 1, 3):
            z3[s, d][0]()
        z_out(0, s)

    def z_gather2(d, s):
        z3[s, d][1]()
        z_out((4 - d) % 4, s)

    def z_forward(d, s):
        (_, from_m), (_, from_p) = z4[s, d]
        from_m()
        z5[s, d][0][0]()
        zs[s, 3, d][0]()
        from_p()
        z5[s, d][1][0]()
        zs[s, 1, d][0]()

    def z_last(d, s):
        for _, wait in z5[s, d]:
            wait()
        zs[s, 2, d][0]()

    for n in range(2):
        k = lax.broadcasted_iota(jnp.int32, (256, RANK), 0)
        rank = lax.shift_right_logical(k, 4) * 32 + (k & 15) + 16 * n
        hit = lax.broadcasted_iota(jnp.int32, (256, RANK), 1) == rank
        onehot[n] = jnp.where(hit, 1.0, 0.0).astype(BF)

    paired, summed, spread, pairs = [], [], [], []

    def left_pair(s):
        for wait in last[s]:
            wait()
        psend[s] = dotb(side[...], bas[s], ((1,), (1,))).astype(BF)
        paired.append(send(psend.at[s], precv.at[s], sib, precv.at[s]))
        pleft[s] = dotb(buf_ref[:, half_of(c)], bas[s], ((1,), (1,)))

    def along_y(d):
        return (r, mod4(y + d))

    def left_rows(core, d):
        return rows_at(core * LOCAL + mod4(y + d) * 96, 96)

    def left_sum(s):
        paired[s]()
        total = pleft[s] + precv[s].astype(F32)
        pleft[s] = total
        chip_left[s] = total.astype(BF)
        summed.append(
            [
                send(
                    chip_left.at[s, rows_at(mod4(y + d) * 96, 96)],
                    yr.at[s, d - 1],
                    along_y(d),
                    yr.at[s, d - 1],
                )
                for d in (2, 1, 3)
            ]
        )

    def left_spread(s):
        for wait in summed[s]:
            wait()
        total = pleft[s, rows_at(y * 96, 96), :]
        for d in range(3):
            total = total + yr[s, d].astype(F32)
        left2[s, left_rows(c, 0), :] = total.astype(BF)
        ref = left2.at[s, left_rows(c, 0)]
        spread.append(
            {d: send(ref, ref, along_y(d), left2.at[s, left_rows(c, -d)]) for d in (2, 1, 3)}
        )
        pairs.append([send(ref, ref, sib, left2.at[s, left_rows(1 - c, 0)])])

    def left_done(s):
        for d in (1, 3, 2):
            spread[s][d]()
            ref = left2.at[s, left_rows(c, -d)]
            pairs[s].append(send(ref, ref, sib, left2.at[s, left_rows(1 - c, -d)]))
        for wait in pairs[s]:
            wait()

    def z_value(d, h, s):
        at = rows_at(mod4(p1 + d) * SEG + (SEG // 2) * h, SEG // 2)
        return dotb(buf2t[at, :], left2[s], ((1,), (0,)))

    ways = (a1p, a1m)
    z_half = [[], []]
    z_full = [[], []]

    def z_first(s):
        for w in range(2):
            zp[s, 2, w] = z_value(2, w, s).astype(BF)
            z_half[s].append(send(zp.at[s, 2, w], zrh.at[s, w], ways[w], zrh.at[s, w]))

    def z_middle(s):
        for w, (d, h) in enumerate(((1, 1), (3, 0))):
            zp[s, d, h] = z_value(d, h, s).astype(BF)
            z_full[s].append(send(zp.at[s, d, h], zrf.at[s, w, h], ways[w], zrf.at[s, w, h]))

    def z_prepare(s):
        for w, (d, h) in enumerate(((1, 0), (3, 1))):
            zl[s, w] = z_value(d, h, s)

    def z_add(s):
        for w, (d, h) in enumerate(((1, 0), (3, 1))):
            z_half[s][w]()
            zp[s, d, h] = (zl[s, w] + zrh[s, w].astype(F32)).astype(BF)
            z_full[s].append(send(zp.at[s, d, h], zrf.at[s, w, h], ways[w], zrf.at[s, w, h]))

    def z_own(s):
        for h in range(2):
            zown[s, h] = z_value(0, h, s)

    add_loaded(0)
    swapped = [send_buffer(0)]
    add_loaded(1)
    swapped.append(send_buffer(1))
    add_loaded(2)
    add_loaded(3)
    pass_on(0)
    turn(0, True)
    pass_on(1)
    turn(1, True)
    forward2(0, 0)
    forward2(1, 0)
    for wait in swapped:
        wait()
    turn(0, False)
    forward2(0, 1)
    turn(1, False)
    forward2(0, 2)
    forward2(0, 3)
    forward2(1, 1)
    forward2(1, 2)
    forward2(1, 3)
    left_pair(0)
    left_sum(0)
    left_pair(1)
    left_sum(1)
    left_spread(0)
    gather_sends = len(sent)
    left_spread(1)
    drain(gather_sends)
    left_done(0)
    z_first(0)
    left_done(1)

    blocks = [(i, j) for i in range(4) for j in range(i, 4)]

    ltrue[...] = (
        dotb(left2[0], onehot[0], ((1,), (0,))) + dotb(left2[1], onehot[1], ((1,), (0,)))
    ).astype(BF)

    def left_block(i):
        return ltrue[:, B * i : B * i + B]

    for b, (i, j) in enumerate(blocks):
        gs[b] = dotb(left_block(i), left_block(j), ((0,), (0,))).astype(BF)
    for b in (10, 11):
        gs[b] = jnp.zeros((B, B), BF)

    def tile(j):
        return pl.ds(lax.rem(j, 4) * 3, 3), rows_at(c * 64 + lax.div(j, 4) * 16, 16)

    gram_in = []
    for e, (dx, dz) in enumerate(plane):
        to = tile(mod4(x + dx) * 4 + mod4(z + dz))
        gram_in.append(send(gs.at[to], gr.at[e], peer(dx, dz), gr.at[e]))
    z_middle(0)
    z_prepare(0)
    z_add(0)
    z_first(1)
    for wait in gram_in:
        wait()
    mine = tile(x * 4 + z)
    gram[mine] = tree([v.astype(F32) for v in [gs[mine]] + [gr[e] for e in range(15)]]).astype(BF)
    gathered = []
    for dx, dz in plane:
        ref = gram.at[mine]
        gathered.append(send(ref, ref, peer(dx, dz), gram.at[tile(source_chip(dx, dz))]))
    z_middle(1)
    z_prepare(1)
    z_own(0)
    z_own(1)
    z_sum1(0)
    z_add(1)
    for wait in gathered:
        wait()
    ref = gram.at[:, rows_at(c * 64, 64)]
    pair_gram = send(ref, ref, sib, gram.at[:, rows_at((1 - c) * 64, 64)])
    pair_gram()

    on = lax.broadcasted_iota(jnp.int32, (B, B), 0) == lax.broadcasted_iota(jnp.int32, (B, B), 1)
    across, down = [], []
    for i in range(4):
        diag = jnp.where(on, gram[blocks.index((i, i))].astype(F32), 0.0)
        across.append(lax.rsqrt(jnp.sum(diag, axis=0, keepdims=True)))
        down.append(lax.rsqrt(jnp.sum(diag, axis=1, keepdims=True)))
    for i in range(4):
        for j in range(4):
            if j < i:
                block = jnp.zeros((B, B), F32)
            else:
                block = gram[blocks.index((i, j))].astype(F32) * down[i] * across[j]
            tmat[B * i : B * i + B, B * j : B * j + B] = block

    steps = {
        (0, 0): lambda: z_sum2(0),
        (0, 5): lambda: z_sum1(1),
        (1, 1): lambda: z_forward(0, 0),
        (1, 4): lambda: z_gather2(1, 0),
        (1, 5): lambda: z_gather2(3, 0),
        (1, 6): lambda: z_gather2(2, 0),
        (2, 0): lambda: z_sum2(1),
        (2, 1): lambda: z_last(0, 0),
        (2, 7): lambda: z_forward(3, 0),
        (3, 0): lambda: z_forward(1, 0),
        (3, 1): lambda: z_forward(2, 0),
        (3, 2): lambda: z_forward(0, 1),
        (3, 3): lambda: z_gather2(1, 1),
        (3, 4): lambda: z_gather2(3, 1),
        (3, 5): lambda: z_gather2(2, 1),
        (3, 7): lambda: z_last(3, 0),
    }

    def hook(k, part):
        for (at, which), step in steps.items():
            if which == part:
                pl.when(k == at)(step)

    sum_sends = len(sent)
    chol_inv(tmat, wmat, hook)
    ri = lax.broadcasted_iota(jnp.int32, (RANK, RANK), 0)
    ci = lax.broadcasted_iota(jnp.int32, (RANK, RANK), 1)
    tmat[...] = jnp.where(ci <= ri, tmat[...], 0.0) * jnp.concatenate(across, axis=1)
    true_hi, true_lo = split(tmat[...])
    shard = (
        dotb(zt_ref[0, sub_rows(p1, p2), :], onehot[0], ((1,), (0,)))
        + dotb(zt_ref[1, sub_rows(p1, p2), :], onehot[1], ((1,), (0,)))
    ).astype(BF)
    right = dotb(shard, true_hi, ((1,), (1,))) + dotb(shard, true_lo, ((1,), (1,)))
    squares = jnp.sum(right * right, axis=0, keepdims=True)
    rows = [squares[:, B * i : B * i + B] for i in range(4)] + [jnp.zeros((4, B), F32)]
    nr1[0] = jnp.concatenate(rows, axis=0)
    norm_in = [
        send(nr1.at[0], nr1.at[e + 1], peer(dx, dz), nr1.at[e + 1])
        for e, (dx, dz) in enumerate(plane)
    ]
    w_hi, w_lo = [
        jnp.concatenate(
            [dotb(w, onehot[n], ((1,), (1,))).astype(BF) for n in range(2)], axis=1
        )
        for w in (true_hi, true_lo)
    ]

    z_last(1, 0)
    z_last(2, 0)
    z_last(0, 1)
    z_forward(3, 1)
    z_forward(1, 1)
    own_left = jnp.concatenate([left2[0, my_rows, :], left2[1, my_rows, :]], axis=1)
    ortho = (dotb(own_left, w_hi, ((1,), (1,))) + dotb(own_left, w_lo, ((1,), (1,)))).astype(BF)
    z_forward(2, 1)
    lhs_ref[:LOCAL, :] = (
        dotb(ortho, w_hi, ((1,), (0,))) + dotb(ortho, w_lo, ((1,), (0,)))
    ).astype(BF)
    drain(sum_sends)
    for wait in norm_in:
        wait()
    nr2[0] = tree([nr1[e] for e in range(16)])
    norm_in = [
        send(nr2.at[0], nr2.at[f + 1], member(dy, dc), nr2.at[f + 1])
        for f, (dy, dc) in enumerate(group)
    ]
    for d in (3, 1, 2):
        z_last(d, 1)
    for wait in norm_in:
        wait()
    total = tree([nr2[f] for f in range(8)])
    total = jnp.concatenate([total[i : i + 1] for i in range(4)], axis=1)
    scale = lax.rsqrt(total + 1e-06)
    sub16 = lax.broadcasted_iota(jnp.int32, (16, RANK), 0)
    lane16 = lax.broadcasted_iota(jnp.int32, (16, RANK), 1)
    pick = jnp.where(lane16 == sub16 + r * 16, scale, 0.0)
    o_hi, o_lo = split(jnp.concatenate([ortho.astype(F32) * scale, pick], axis=0))
    lhs_ref[LOCAL:, :] = (
        dotb(o_hi, w_hi, ((1,), (0,)))
        + (dotb(o_hi, w_lo, ((1,), (0,))) + dotb(o_lo, w_hi, ((1,), (0,))))
    ).astype(BF)
    for _, wait in zs.values():
        wait()
    for wait in sent:
        wait()


def gather_call(momentum, gradient, basis):
    anyspace = pl.BlockSpec(memory_space=pl.ANY)
    vmem = pl.BlockSpec(memory_space=pltpu.VMEM)
    scratch = [
        ((2, LOCAL, PART), BF),
        ((2, LOCAL, PART), BF),
        ((LOCAL, HALF), BF),
        ((HALF, 2 * LOCAL), BF),
        ((2, 256, HALF), BF),
        ((2, LOCAL, 256), F32),
        ((2, LOCAL, 256), BF),
        ((2, LOCAL, 256), BF),
        ((2, LOCAL, 256), BF),
        ((2, 3, 96, 256), BF),
        ((2, 2 * LOCAL, 256), BF),
        ((12, B, B), BF),
        ((15, 3, 16, B), BF),
        ((12, B, B), BF),
        ((RANK, RANK), F32),
        ((B, B), F32),
        ((2, 4, 2, SEG // 2, 256), BF),
        ((2, 2, SEG // 2, 256), F32),
        ((2, 2, SEG // 2, 256), F32),
        ((2, 2, SEG // 2, 256), BF),
        ((2, 2, 2, SEG // 2, 256), BF),
        ((2, 3, SUB, 256), BF),
        ((16, 8, B), F32),
        ((8, 8, B), F32),
        ((2, 256, RANK), BF),
        ((2 * LOCAL, RANK), BF),
    ]
    return pl.pallas_call(
        gather_kernel,
        out_shape=(
            pltpu.VMEM((LOCAL, COLS), BF),
            pltpu.VMEM((2, COLS, 256), BF),
            pltpu.VMEM((2 * LOCAL + 16, RANK), BF),
        ),
        in_specs=[anyspace] * 3,
        out_specs=(vmem,) * 3,
        scratch_shapes=[pltpu.VMEM(s, t) for s, t in scratch]
        + [
            pltpu.SemaphoreType.DMA((9,)),
            pltpu.SemaphoreType.DMA((N_SEMS,)),
            pltpu.SemaphoreType.DMA((N_SEMS,)),
        ],
        compiler_params=pltpu.CompilerParams(
            collective_id=0, has_side_effects=True, vmem_limit_bytes=44 << 20
        ),
        name="project",
    )(momentum, gradient, basis)


def apply_kernel(buf_ref, zt_ref, lhs_ref, mom_hbm, bas_hbm, upd_hbm, mom, bas, upd, sem):
    factor = math.sqrt(ROWS * WIDTH / RANK)
    copies = []

    def write(n, src, dst):
        copies.append(pltpu.make_async_copy(src, dst, sem.at[n]))
        copies[-1].start()

    for n in range(COLS // 512):
        at = pl.ds(512 * n, 512)
        prod = dotb(lhs_ref[:, :256], zt_ref[0, at, :], ((1,), (1,)))
        prod = prod + dotb(lhs_ref[:, 256:], zt_ref[1, at, :], ((1,), (1,)))
        mom[:, at] = (buf_ref[:, at].astype(F32) - 0.2 * prod[:LOCAL]).astype(BF)
        write(2 * n, mom.at[:, at], mom_hbm.at[:, at])
        upd[:, at] = (factor * prod[LOCAL : 2 * LOCAL]).astype(BF)
        write(2 * n + 1, upd.at[:, at], upd_hbm.at[:, at])
        bas[:, at] = prod[2 * LOCAL :].astype(BF)
    write(2 * (COLS // 512), bas, bas_hbm)
    for copy in copies:
        copy.wait()


def apply_call(buf, zt, lhs):
    held = [pltpu.with_memory_space_constraint(v, pltpu.VMEM) for v in (buf, zt, lhs)]
    return pl.pallas_call(
        apply_kernel,
        out_shape=(
            jax.ShapeDtypeStruct((LOCAL, COLS), BF),
            jax.ShapeDtypeStruct((16, COLS), BF),
            jax.ShapeDtypeStruct((LOCAL, COLS), BF),
        ),
        in_specs=[pl.BlockSpec(memory_space=pltpu.VMEM)] * 3,
        out_specs=[pl.BlockSpec(memory_space=pl.ANY)] * 3,
        scratch_shapes=[
            pltpu.VMEM((LOCAL, COLS), BF),
            pltpu.VMEM((16, COLS), BF),
            pltpu.VMEM((LOCAL, COLS), BF),
            pltpu.SemaphoreType.DMA((1 + 2 * (COLS // 512),)),
        ],
        compiler_params=pltpu.CompilerParams(vmem_limit_bytes=30 << 20),
        name="apply",
    )(*held)


def local(momentum, gradient, basis):
    return apply_call(*gather_call(momentum, gradient, basis))


def solution(mesh):
    return jax.shard_map(
        local,
        mesh=mesh,
        in_specs=(P("rows", "cols"), P("rows", "cols"), P("rows", "cols")),
        out_specs=(P("rows", "cols"), P("rows", "cols"), P("rows", "cols")),
        check_vma=False,
    )
```
